128 devices in a mesh: surf: 32 (over z, y, core), vol: 4 (over x).
Axes of the slice: x: 4, y: 4, z: 4, core: 2. Of those that a mesh axis runs over, the one named last changes fastest.
Arguments:
- casting: bfloat16 [131072, 128], P(('surf', 'vol')), may hold values from -5 to 5, as said below
- owner: int32 [131072, 1], P(('surf', 'vol')), may hold values from 0 to 127; in each aligned block of 1024 rows (0 to 1023, 1024 to 2047, ...) at most 32 rows name the same one
- face_id: int32 [131072], P(('surf', 'vol')), may hold values from 0 to 2047
- mold_faces: bfloat16 [262144, 128], P(('surf', 'vol')), may hold values from -5 to 5, as said below
- mortar_d: bfloat16 [64, 64], replicated, may hold values from -0.75 to 0.75
- mortar_m: bfloat16 [64, 64], replicated, may hold values from -0.75 to 0.75
- conduct: bfloat16 [128, 128], replicated, may hold values from -0.5 to 0.5
- volume: bfloat16 [262144, 128], P(('surf', 'vol')), may hold values from -6 to 6
Outputs:
- casting_out: bfloat16 [131072, 128], P(('surf', 'vol'))
- mold_out: bfloat16 [262144, 128], P(('surf', 'vol'))
The draws below stay inside these ranges and needn't reach their ends.
Inputs may be any that keep to these rules, and one draw needn't show every extreme that they name: Among the 1024 rows of one device no owner is named more than 32 times, a bound that some block reaches. `casting`: temperatures lie within -5 to 5; conductances lie within 0.3 to 3. `mold_faces`: temperatures lie within -5 to 5; area weights lie within 0.3 to 3.
All inputs are finite; a program needn't handle non-finite values.
Results may differ from the reference program's by a relative error of at most 0.0055.
Values may be sent and summed in bfloat16 or wider, within the bound.
A program may use at most 64 MiB of HBM per device.

```python
import math
import jax
import jax.numpy as jnp
import numpy as np

NODES = 64
ROW = 128
SEG_DEV = 1024
FACE_DEV = 2048
CAP = 32
SEGS = 131072
FACES = 262144
N_SURF = 32
N_VOL = 4
DEVICES = 128


def surface_rows(key, count):
    first, second = jax.random.split(jax.random.fold_in(key, 7))
    temps = jnp.clip(jax.random.normal(first, (count, NODES), jnp.float32), -5.0, 5.0)
    coeffs = jnp.exp(jax.random.uniform(second, (count, NODES), jnp.float32, math.log(0.3), math.log(3.0)))
    return jnp.concatenate([temps, coeffs], axis=1).astype(jnp.bfloat16)


def draw_casting(key, part):
    return surface_rows(key, SEGS)


def draw_mold_faces(key, part):
    return surface_rows(jax.random.fold_in(key, 11), FACES)


def plant(entries, stream_key, least, top_value):
    extent = entries.shape
    index_at = [jax.random.randint(jax.random.fold_in(stream_key, axis), (), 0, extent[axis]) for axis in range(len(extent))]
    entries = entries.at[tuple(index_at)].set(least)
    longest = extent.index(max(extent))
    index_at[longest] = (index_at[longest] + 1) % extent[longest]
    return entries.at[tuple(index_at)].set(top_value)


def block_scale(key, extent, shards, low, largest):
    def one(position, shards_of):
        steps = jax.random.uniform(jax.random.fold_in(jax.random.fold_in(key, 6), position), (shards_of,), jnp.float32, low / len(shards), largest / len(shards))
        return jnp.repeat(jnp.exp(steps), extent[position] // shards_of).reshape((-1,) + (1,) * (len(extent) - position - 1))

    factor_of = one(*shards[0])
    for cut in shards[1:]:
        factor_of = factor_of * one(*cut)
    return factor_of


def routed_block(own_key, own, number, rows, amount, top, reach, skew):
    sequence = jax.random.permutation(own_key, amount)
    packed, ordinary = shares(amount, rows * top, reach, skew, True), shares(amount, rows * top, reach, skew, False)
    places = jnp.arange(amount)

    def named(tallies, offset_by):
        used = int((tallies > 0).sum())
        fixed = max(1, used // 4)
        moved = fixed + (places - fixed + offset_by * (used - fixed)) % max(1, amount - fixed)
        return jnp.zeros((amount,), jnp.int32).at[sequence[jnp.where(places < fixed, places, moved)]].set(jnp.asarray(tallies, jnp.int32))

    tallies = jnp.where(number % 4 == 0, named(packed, number // 4), named(ordinary, number - number // 4 - 1))
    mixed = jax.random.permutation(jax.random.fold_in(own, 3), amount)
    giver, taker = mixed[0:amount // 2 * 2:2], mixed[1:amount // 2 * 2:2]
    room = jnp.minimum(tallies[giver] - 1, reach - tallies[taker]) // 2
    room = jnp.where((giver == sequence[0]) | (taker == sequence[0]) | (tallies[taker] == 0), 0, jnp.maximum(room, 0))
    moved = jax.random.randint(jax.random.fold_in(own, 4), (amount // 2,), 0, 1 << 20) % (room + 1)
    tallies = tallies.at[giver].add(-moved).at[taker].add(moved)
    members = jnp.searchsorted(jnp.cumsum(tallies), jnp.arange(rows * top), side="right").astype(jnp.int32)
    table = members.reshape(top, rows).T
    table = table[jax.random.permutation(jax.random.fold_in(own, 1), rows)]
    offset_by = jax.random.randint(jax.random.fold_in(own, 2), (rows, 1), 0, top)
    return jnp.take_along_axis(table, (jnp.arange(top)[None, :] + offset_by) % top, axis=1)


def shares(amount, total, most, skew, full):
    weights = [(1 << 20) // math.isqrt(rank ** skew) + 1 for rank in range(1, amount + 1)]
    largest = most if full else min(most, max(-(-total // amount), total * weights[0] // sum(weights)))
    least = 1 if total - largest >= amount - 1 else 0
    given, spare = [largest] + [least] * (amount - 1), total - largest - least * (amount - 1)
    while spare > 0:
        candidates = [i for i in range(1, amount) if given[i] < largest] or [i for i in range(1, amount) if given[i] < most]
        pool, left = sum([weights[i] for i in candidates]), spare
        for i in candidates:
            extra = min(most - given[i], max(1, left * weights[i] // pool), spare)
            given[i] = given[i] + extra
            spare = spare - extra
    return np.array(given)


def noise(rng, shape, scale, reach, cuts=(), held_as=jnp.bfloat16):
    loudness = block_scale(rng, shape, cuts, -0.22, 0.18) if cuts else 1.0
    values = jax.random.normal(rng, shape, jnp.float32) * scale * loudness
    return jnp.minimum(jnp.maximum(values, -reach), reach).astype(held_as)


def setup_inputs(seed: int = 0) -> dict:
    keys = jax.random.split(jax.random.key(seed), 9)
    casting = draw_casting(jax.random.fold_in(keys[8], 71), 0)
    owner_keys = jax.random.split(jax.random.fold_in(keys[1], 1), SEGS // SEG_DEV)
    owner_turns = jax.random.permutation(jax.random.fold_in(keys[1], 3), SEGS // SEG_DEV)
    owner = jax.vmap(lambda own, number: routed_block(jax.random.fold_in(keys[1], 2), own, number, SEG_DEV, DEVICES, 1, CAP, 2))(owner_keys, owner_turns).reshape((SEGS, 1))
    face_id = plant(jax.random.randint(keys[2], (SEGS,), 0, FACE_DEV), jax.random.fold_in(keys[2], 1), 0, FACE_DEV - 1).astype(jnp.int32)
    mold_faces = draw_mold_faces(jax.random.fold_in(keys[8], 71), 0)
    mortar_d = noise(keys[4], (NODES, NODES), NODES ** -0.5, 0.75)
    mortar_m = noise(keys[5], (NODES, NODES), NODES ** -0.5, 0.75)
    conduct = noise(keys[6], (ROW, ROW), ROW ** -0.5, 0.5)
    volume = noise(keys[7], (FACES, ROW), 1.0, 6.0, ((0, 128),))
    return dict(casting=casting, owner=owner, face_id=face_id, mold_faces=mold_faces, mortar_d=mortar_d, mortar_m=mortar_m, conduct=conduct, volume=volume)


relax = 0.5


def reference(casting, owner, face_id, mold_faces, mortar_d, mortar_m, conduct, volume):
    paired = owner[:, 0].astype(jnp.int32) * FACE_DEV + face_id.astype(jnp.int32)
    mold_rows = mold_faces[paired]
    stacked = jnp.concatenate([mortar_d.T, -mortar_m.T], axis=0)
    joined = jnp.concatenate([mortar_d, mortar_m], axis=1)
    pair_rows = jnp.concatenate([casting[:, :NODES], mold_rows[:, :NODES]], axis=1)
    gap_jump = jnp.dot(pair_rows, stacked, preferred_element_type=jnp.float32)
    heat_flux = (casting[:, NODES:].astype(jnp.float32) * mold_rows[:, NODES:].astype(jnp.float32) * gap_jump).astype(jnp.bfloat16)
    projected = jnp.dot(heat_flux, joined, preferred_element_type=jnp.float32)
    casting_out = jnp.concatenate([projected[:, :NODES], gap_jump], axis=1).astype(jnp.bfloat16)
    gained = projected[:, NODES:].astype(jnp.bfloat16)
    totals = jax.ops.segment_sum(gained.astype(jnp.float32), paired, num_segments=FACES).astype(jnp.bfloat16)
    quarter = FACE_DEV // N_VOL
    placed = totals.reshape(N_SURF, N_VOL, N_VOL, quarter, NODES).transpose(0, 2, 1, 3, 4).reshape(FACES, NODES)
    heat = jnp.dot(volume, conduct, preferred_element_type=jnp.float32)
    inject = jnp.concatenate([placed.astype(jnp.float32), jnp.zeros((FACES, NODES), jnp.float32)], axis=1)
    mold_out = (volume.astype(jnp.float32) + relax * (inject - heat)).astype(jnp.bfloat16)
    return casting_out, mold_out
```

```python
import functools

import jax
import jax.numpy as jnp
from jax import lax
from jax.experimental import pallas as pl
from jax.experimental.pallas import tpu as pltpu
from jax.sharding import PartitionSpec as P

MESH = pl.DeviceIdType.MESH
BF = jnp.bfloat16
F32 = jnp.float32
I32 = jnp.int32

PEERS = 128
PER = 32
BATCH = 16
BATCHES = PEERS // BATCH
SLOTS = BATCH * PER
NODES = 64
ROW = 128
SEGS = 1024
FACES = 2048
QUARTER = FACES // 4


def iota(shape, dim):
    return lax.broadcasted_iota(I32, shape, dim)


def kernel(
    owner_ref,
    face_ref,
    d_ref,
    m_ref,
    conduct_ref,
    casting_hbm,
    mold_hbm,
    volume_hbm,
    cout_hbm,
    mout_hbm,
    casting_v,
    mold_v,
    volume_v,
    send_v,
    recv_v,
    ans_v,
    back_v,
    ids_send,
    ids_recv,
    wgap_v,
    mfour_v,
    wcond_v,
    tile_v,
    spread_v,
    row8_v,
    slotrep_v,
    totals_v,
    quarter_v,
    placed_v,
    acc_v,
    cout_v,
    mout_v,
    load_sem,
    out_sem,
    row_sem,
    id_sem,
    ans_sem,
    tot_sem,
    sent_sem,
):
    surf = lax.axis_index("surf")
    x = lax.axis_index("vol")
    z, y, c = surf // 8, lax.rem(surf // 2, 4), lax.rem(surf, 2)

    def peer(g, i, sign):
        dz, dy = i // 4, i % 4
        pz = lax.rem(z + 4 + sign * dz, 4)
        py = lax.rem(y + 4 + sign * dy, 4)
        px = lax.rem(x + 16 + sign * (g // 2 + dz + dy), 4)
        pc = lax.rem(c + lax.rem(g, 2) + dz, 2)
        return (pz * 8 + py * 2 + pc, px)

    def each_peer(g, act, own):
        for i in range(BATCH):
            if i == 0:
                pl.when(g > 0)(functools.partial(act, g, i))
                if own is not None:
                    pl.when(g == 0)(own)
            else:
                act(g, i)

    loads = [
        pltpu.make_async_copy(casting_hbm, casting_v, load_sem.at[0]),
        pltpu.make_async_copy(mold_hbm.at[pl.ds(0, 1024)], mold_v.at[:, pl.ds(0, ROW)], load_sem.at[1]),
        pltpu.make_async_copy(mold_hbm.at[pl.ds(1024, 1024)], mold_v.at[:, pl.ds(ROW, ROW)], load_sem.at[2]),
        pltpu.make_async_copy(volume_hbm, volume_v, load_sem.at[3]),
    ]
    for load in loads:
        load.start()

    barrier = pltpu.get_barrier_semaphore()

    def greet(g, _):
        def one(g, i):
            pl.semaphore_signal(barrier, inc=1, device_id=peer(g, i, 1), device_id_type=MESH)

        each_peer(g, one, None)
        return 0

    lax.fori_loop(0, BATCHES, greet, 0)

    owner = owner_ref[...]
    dx = (owner & 3) - x & 3
    dc = (owner >> 2 & 1) - c & 1
    dy = (owner >> 3 & 3) - y & 3
    dz = (owner >> 5 & 3) - z & 3
    order = (dx - dz - dy & 3) * 32 + (dc - dz & 1) * 16 + dz * 4 + dy
    down, lane = iota((ROW, ROW), 0), iota((ROW, ROW), 1)
    before = jnp.concatenate([(down < lane).astype(F32), jnp.ones((ROW, ROW), F32)], axis=1).astype(BF)
    hits, sofar = [], jnp.zeros((PEERS, ROW), F32)
    for b in range(8):
        hit = down == order[b : b + 1, :]
        hits.append(hit.astype(F32).astype(BF))
        count = jnp.dot(hits[b], before, preferred_element_type=F32)
        rank = jnp.sum(jnp.where(hit, count[:, :ROW] + sofar, 0.0), axis=0, keepdims=True)
        sofar = sofar + count[:, ROW:]
        row8_v[b : b + 1, :] = rank
    slot8 = (order * PER).astype(F32) + row8_v[...]
    row8_v[...] = slot8
    slot_t = slot8.T
    face_t = face_ref[...].astype(F32).T
    table = jnp.zeros((PEERS, ROW), F32)
    for b in range(8):
        slot = jnp.broadcast_to(slot_t[:, b : b + 1], (ROW, ROW)).astype(I32)
        face = jnp.broadcast_to(face_t[:, b : b + 1], (ROW, ROW)).astype(I32)
        slotrep_v[pl.ds(b * ROW, ROW), :] = slot
        part = jnp.where(lane < 32, face & 255, jnp.where(lane < 64, face >> 8 & 3, face >> 10))
        part = jnp.where(((lane & 31) == (slot & 31)) & (lane < 96), part, 0)
        table = table + jnp.dot(hits[b], part.astype(F32).astype(BF), preferred_element_type=F32)
    ids_send[...] = table

    wgap_v[...] = jnp.zeros_like(wgap_v)
    wgap_v[NODES:, 0:NODES] = d_ref[...]
    wgap_v[NODES:, ROW : ROW + NODES] = -m_ref[...]
    mtwo = jnp.concatenate([m_ref[...], m_ref[...]], axis=1)
    mfour_v[...] = jnp.zeros_like(mfour_v)
    mfour_v[NODES:, 0:ROW] = mtwo
    mfour_v[NODES:, ROW:] = mtwo
    for half in range(2):
        pick = jnp.where((down == lane + half * NODES) & (lane < NODES), 0.5, 0.0)
        wcond_v[half, 0:ROW, :] = pick.astype(BF)
        wcond_v[half, ROW:, :] = (conduct_ref[...].astype(F32) * -0.5).astype(BF)
    wide_d, wide_l = iota((ROW, SLOTS), 0), iota((ROW, SLOTS), 1)
    tile = jnp.where(wide_d == (wide_l & 31), 1.0, jnp.where(wide_d == (wide_l & 31) + 64, 256.0, 0.0))
    tile_v[...] = tile.astype(BF)
    down2, lane2 = iota((ROW, 2 * ROW), 0), iota((ROW, 2 * ROW), 1)
    part2 = down2 >> 5
    spread = jnp.where(
        lane2 < ROW,
        jnp.where(part2 == 0, 1.0, jnp.where(part2 == 1, 256.0, 0.0)),
        jnp.where(part2 == 1, 1.0, jnp.where(part2 == 2, 4.0, 0.0)),
    )
    spread_v[...] = spread.astype(BF)
    totals_v[...] = jnp.zeros_like(totals_v)
    acc_v[...] = jnp.zeros_like(acc_v)

    loads[0].wait()

    def pack(g, _):
        want = iota((SLOTS, ROW), 0) + g * SLOTS
        want = want.astype(F32)
        pick = jnp.concatenate(
            [(want == row8_v[b : b + 1, :]).astype(F32).astype(BF) for b in range(8)], axis=1
        )
        rows = jnp.dot(pick, casting_v[...], preferred_element_type=F32).astype(BF)
        send_v[pl.ds(g * BATCH, BATCH)] = rows.reshape(BATCH, PER, ROW)
        return 0

    lax.fori_loop(0, BATCHES, pack, 0)
    pl.semaphore_wait(barrier, PEERS - 1)

    def send(g, _):
        def one(g, i):
            j = g * BATCH + i
            to = peer(g, i, 1)
            pltpu.make_async_remote_copy(
                src_ref=ids_send.at[pl.ds(j, 1)],
                dst_ref=ids_recv.at[pl.ds(j, 1)],
                send_sem=sent_sem.at[0],
                recv_sem=id_sem.at[g],
                device_id=to,
                device_id_type=MESH,
            ).start()
            pltpu.make_async_remote_copy(
                src_ref=send_v.at[j],
                dst_ref=recv_v.at[j],
                send_sem=sent_sem.at[1],
                recv_sem=row_sem.at[g],
                device_id=to,
                device_id_type=MESH,
            ).start()

        def own():
            pltpu.make_async_copy(ids_send.at[pl.ds(0, 1)], ids_recv.at[pl.ds(0, 1)], id_sem.at[0]).start()
            pltpu.make_async_copy(send_v.at[0], recv_v.at[0], row_sem.at[0]).start()

        each_peer(g, one, own)
        return 0

    lax.fori_loop(0, BATCHES, send, 0)
    loads[1].wait()
    loads[2].wait()

    def wait_for(ref, sem):
        pltpu.make_async_copy(ref, ref, sem).wait()

    def settle(g, _):
        span = pl.ds(pl.multiple_of(g * BATCH, BATCH), BATCH)
        wait_for(ids_recv.at[span], id_sem.at[g])
        wait_for(recv_v.at[span], row_sem.at[g])
        ids = ids_recv[span, :]
        across = jnp.dot(ids.astype(BF), tile_v[...], preferred_element_type=F32)
        mine = iota((BATCH, SLOTS), 0) == iota((BATCH, SLOTS), 1) >> 5
        across = jnp.sum(jnp.where(mine, across, 0.0), axis=0, keepdims=True)
        keep = iota((PER, ROW), 0) == (iota((PER, ROW), 1) & 31)
        spaced = jnp.where(keep[None], jnp.broadcast_to(ids[:, None, :], (BATCH, PER, ROW)), 0.0)
        spaced = spaced.reshape(SLOTS, ROW).astype(BF)
        both = jnp.dot(spaced, spread_v[...], preferred_element_type=F32)
        low, high = both[:, :ROW], both[:, ROW:]
        lanes = iota((SLOTS, ROW), 1).astype(F32)
        pick = jnp.concatenate([(low - t * ROW == lanes).astype(F32).astype(BF) for t in range(8)], axis=1)
        found = jnp.dot(pick, mold_v[...], preferred_element_type=F32)
        upper = high >= 4.0
        faces = jnp.where(upper, found[:, ROW:], found[:, :ROW]).astype(BF)
        rows = recv_v[span].reshape(SLOTS, ROW)
        pair = jnp.concatenate([rows, faces], axis=1)
        gap = lax.dot_general(pair, wgap_v[...], (((1,), (1,)), ((), ())), preferred_element_type=F32)
        flux = (rows.astype(F32) * faces.astype(F32) * gap).astype(BF)
        back = jnp.dot(flux, wgap_v[:, :ROW], preferred_element_type=F32)
        answer = (back + gap).astype(BF)
        ans_v[span] = answer.reshape(BATCH, PER, ROW)

        def one(g, i):
            j = g * BATCH + i
            pltpu.make_async_remote_copy(
                src_ref=ans_v.at[j],
                dst_ref=back_v.at[j],
                send_sem=sent_sem.at[2],
                recv_sem=ans_sem.at[g],
                device_id=peer(g, i, -1),
                device_id_type=MESH,
            ).start()

        def own():
            pltpu.make_async_copy(ans_v.at[0], back_v.at[0], ans_sem.at[0]).start()

        each_peer(g, one, own)
        gain = jnp.dot(flux, mfour_v[...], preferred_element_type=F32)
        column = jnp.where(upper, high - 4.0, high)
        block = (iota((SLOTS, ROW), 1) >> 6).astype(F32)
        gain = jnp.concatenate(
            [
                jnp.where(column == block, gain[:, :ROW], 0.0).astype(BF),
                jnp.where(column == block + 2.0, gain[:, ROW:], 0.0).astype(BF),
            ],
            axis=1,
        )
        put = (iota((SLOTS, SLOTS), 0).astype(F32) == across).astype(F32).astype(BF)
        totals_v[...] += jnp.dot(put, gain, preferred_element_type=F32)
        return 0

    lax.fori_loop(0, BATCHES, settle, 0)

    for q in range(4):
        rows = slice((q // 2) * 256, (q // 2) * 256 + 256)
        cols = slice((q % 2) * ROW, (q % 2) * ROW + ROW)
        quarter_v[q] = totals_v[rows, cols].astype(BF)
    for d in range(4):
        v = lax.rem(x + d, 4)
        if d == 0:
            pltpu.make_async_copy(quarter_v.at[v], placed_v.at[x], tot_sem.at[0]).start()
        else:
            pltpu.make_async_remote_copy(
                src_ref=quarter_v.at[v],
                dst_ref=placed_v.at[x],
                send_sem=sent_sem.at[3],
                recv_sem=tot_sem.at[0],
                device_id=(surf, v),
                device_id_type=MESH,
            ).start()

    def collect(g, _):
        span = pl.ds(pl.multiple_of(g * BATCH, BATCH), BATCH)
        wait_for(back_v.at[span], ans_sem.at[g])
        lanes = iota((SEGS, ROW), 1) + g * SLOTS
        slots = slotrep_v[...]
        pick = jnp.concatenate(
            [(slots == lanes + t * ROW).astype(F32).astype(BF) for t in range(SLOTS // ROW)], axis=1
        )
        acc_v[...] += jnp.dot(pick, back_v[span].reshape(SLOTS, ROW), preferred_element_type=F32)
        return 0

    lax.fori_loop(0, BATCHES - 2, collect, 0)

    loads[3].wait()
    wait_for(placed_v, tot_sem.at[0])
    for u in range(4):
        for half in range(2):
            rows = slice(u * QUARTER + half * 256, u * QUARTER + half * 256 + 256)
            volume = volume_v[rows, :]
            both = jnp.concatenate([placed_v[u], volume], axis=1)
            change = jnp.dot(both, wcond_v[half], preferred_element_type=F32)
            mout_v[rows, :] = (volume.astype(F32) + change).astype(BF)
    mold_store = pltpu.make_async_copy(mout_v, mout_hbm, out_sem.at[0])
    mold_store.start()

    lax.fori_loop(BATCHES - 2, BATCHES, collect, 0)
    cout_v[...] = acc_v[...].astype(BF)
    casting_store = pltpu.make_async_copy(cout_v, cout_hbm, out_sem.at[1])
    casting_store.start()
    wait_for(ids_send.at[pl.ds(1, PEERS - 1)], sent_sem.at[0])
    wait_for(send_v.at[pl.ds(1, PEERS - 1)], sent_sem.at[1])
    wait_for(ans_v.at[pl.ds(1, PEERS - 1)], sent_sem.at[2])
    wait_for(quarter_v.at[pl.ds(0, 3)], sent_sem.at[3])
    mold_store.wait()
    casting_store.wait()


def local(casting, owner, face_id, mold_faces, mortar_d, mortar_m, conduct, volume):
    vmem = pl.BlockSpec(memory_space=pltpu.VMEM)
    hbm = pl.BlockSpec(memory_space=pl.ANY)
    slots = (PEERS, PER, ROW)
    return pl.pallas_call(
        kernel,
        out_shape=(
            jax.ShapeDtypeStruct((SEGS, ROW), BF),
            jax.ShapeDtypeStruct((FACES, ROW), BF),
        ),
        in_specs=[vmem] * 5 + [hbm] * 3,
        out_specs=(hbm, hbm),
        scratch_shapes=[
            pltpu.VMEM((SEGS, ROW), BF),
            pltpu.VMEM((1024, 2 * ROW), BF),
            pltpu.VMEM((FACES, ROW), BF),
            pltpu.VMEM(slots, BF),
            pltpu.VMEM(slots, BF),
            pltpu.VMEM(slots, BF),
            pltpu.VMEM(slots, BF),
            pltpu.VMEM((PEERS, ROW), F32),
            pltpu.VMEM((PEERS, ROW), F32),
            pltpu.VMEM((ROW, 2 * ROW), BF),
            pltpu.VMEM((ROW, 2 * ROW), BF),
            pltpu.VMEM((2, 2 * ROW, ROW), BF),
            pltpu.VMEM((ROW, SLOTS), BF),
            pltpu.VMEM((ROW, 2 * ROW), BF),
            pltpu.VMEM((8, ROW), F32),
            pltpu.VMEM((SEGS, ROW), I32),
            pltpu.VMEM((SLOTS, 2 * ROW), F32),
            pltpu.VMEM((4, 256, ROW), BF),
            pltpu.VMEM((4, 256, ROW), BF),
            pltpu.VMEM((SEGS, ROW), F32),
            pltpu.VMEM((SEGS, ROW), BF),
            pltpu.VMEM((FACES, ROW), BF),
            pltpu.SemaphoreType.DMA((4,)),
            pltpu.SemaphoreType.DMA((2,)),
            pltpu.SemaphoreType.DMA((BATCHES,)),
            pltpu.SemaphoreType.DMA((BATCHES,)),
            pltpu.SemaphoreType.DMA((BATCHES,)),
            pltpu.SemaphoreType.DMA((1,)),
            pltpu.SemaphoreType.DMA((4,)),
        ],
        compiler_params=pltpu.CompilerParams(
            collective_id=0, has_side_effects=True, vmem_limit_bytes=40 * 2**20
        ),
        cost_estimate=pl.CostEstimate(
            flops=2 * 4096 * 1024 * 1024, bytes_accessed=2 * 2**20, transcendentals=0
        ),
    )(
        owner.reshape(8, ROW),
        face_id.reshape(8, ROW),
        mortar_d,
        mortar_m,
        conduct,
        casting,
        mold_faces,
        volume,
    )


def solution(mesh):
    rows, flat = P(("surf", "vol"), None), P(("surf", "vol"))
    return jax.shard_map(
        local,
        mesh=mesh,
        in_specs=(rows, rows, flat, rows, P(), P(), P(), rows),
        out_specs=(rows, rows),
        check_vma=False,
    )
```

```python
import functools

import jax
import jax.numpy as jnp
from jax import lax
from jax.experimental import pallas as pl
from jax.experimental.pallas import tpu as pltpu
from jax.sharding import PartitionSpec as P

MESH = pl.DeviceIdType.MESH
BF = jnp.bfloat16
F32 = jnp.float32
I32 = jnp.int32

PEERS = 128
PER = 32
BATCH = 16
BATCHES = PEERS // BATCH
SLOTS = BATCH * PER
NODES = 64
ROW = 128
SEGS = 1024
FACES = 2048
QUARTER = FACES // 4


def iota(shape, dim):
    return lax.broadcasted_iota(I32, shape, dim)


def kernel(
    owner_hbm,
    face_hbm,
    d_hbm,
    m_hbm,
    conduct_hbm,
    casting_hbm,
    mold_hbm,
    volume_hbm,
    cout_hbm,
    mout_hbm,
    owner_ref,
    face_ref,
    d_ref,
    m_ref,
    conduct_ref,
    casting_v,
    mold_v,
    volume_v,
    send_v,
    recv_v,
    ans_v,
    back_v,
    ids_send,
    ids_recv,
    wgap_v,
    mfour_v,
    wcond_v,
    tile_v,
    spread_v,
    row8_v,
    slotrep_v,
    totals_v,
    quarter_v,
    placed_v,
    acc_v,
    cout_v,
    mout_v,
    load_sem,
    out_sem,
    row_sem,
    id_sem,
    ans_sem,
    tot_sem,
    sent_sem,
):
    surf = lax.axis_index("surf")
    x = lax.axis_index("vol")
    z, y, c = surf // 8, lax.rem(surf // 2, 4), lax.rem(surf, 2)

    def peer(g, i, sign):
        dz, dy = i // 4, i % 4
        pz = lax.rem(z + 4 + sign * dz, 4)
        py = lax.rem(y + 4 + sign * dy, 4)
        px = lax.rem(x + 16 + sign * (g // 2 + dz + dy), 4)
        pc = lax.rem(c + lax.rem(g, 2) + dz, 2)
        return (pz * 8 + py * 2 + pc, px)

    def each_peer(g, act, own):
        for i in range(BATCH):
            if i == 0:
                pl.when(g > 0)(functools.partial(act, g, i))
                if own is not None:
                    pl.when(g == 0)(own)
            else:
                act(g, i)

    small = [
        pltpu.make_async_copy(source, place, load_sem.at[4 + n])
        for n, (source, place) in enumerate(
            [
                (owner_hbm, owner_ref),
                (face_hbm, face_ref),
                (d_hbm, d_ref),
                (m_hbm, m_ref),
                (conduct_hbm, conduct_ref),
            ]
        )
    ]
    loads = [
        pltpu.make_async_copy(casting_hbm, casting_v, load_sem.at[0]),
        pltpu.make_async_copy(mold_hbm.at[pl.ds(0, 1024)], mold_v.at[:, pl.ds(0, ROW)], load_sem.at[1]),
        pltpu.make_async_copy(mold_hbm.at[pl.ds(1024, 1024)], mold_v.at[:, pl.ds(ROW, ROW)], load_sem.at[2]),
        pltpu.make_async_copy(volume_hbm, volume_v, load_sem.at[3]),
    ]
    for load in small + loads:
        load.start()

    barrier = pltpu.get_barrier_semaphore()

    def greet(g, _):
        def one(g, i):
            pl.semaphore_signal(barrier, inc=1, device_id=peer(g, i, 1), device_id_type=MESH)

        each_peer(g, one, None)
        return 0

    lax.fori_loop(0, BATCHES, greet, 0)

    small[0].wait()
    owner = owner_ref[...]
    dx = (owner & 3) - x & 3
    dc = (owner >> 2 & 1) - c & 1
    dy = (owner >> 3 & 3) - y & 3
    dz = (owner >> 5 & 3) - z & 3
    order = (dx - dz - dy & 3) * 32 + (dc - dz & 1) * 16 + dz * 4 + dy
    down, lane = iota((ROW, ROW), 0), iota((ROW, ROW), 1)
    before = jnp.concatenate([(down < lane).astype(F32), jnp.ones((ROW, ROW), F32)], axis=1).astype(BF)
    hits, sofar = [], jnp.zeros((PEERS, ROW), F32)
    for b in range(8):
        hit = down == order[b : b + 1, :]
        hits.append(hit.astype(F32).astype(BF))
        count = jnp.dot(hits[b], before, preferred_element_type=F32)
        rank = jnp.sum(jnp.where(hit, count[:, :ROW] + sofar, 0.0), axis=0, keepdims=True)
        sofar = sofar + count[:, ROW:]
        row8_v[b : b + 1, :] = rank
    slot8 = (order * PER).astype(F32) + row8_v[...]
    row8_v[...] = slot8
    slot_t = slot8.T
    small[1].wait()
    face_t = face_ref[...].astype(F32).T
    table = jnp.zeros((PEERS, ROW), F32)
    for b in range(8):
        slot = jnp.broadcast_to(slot_t[:, b : b + 1], (ROW, ROW)).astype(I32)
        face = jnp.broadcast_to(face_t[:, b : b + 1], (ROW, ROW)).astype(I32)
        slotrep_v[pl.ds(b * ROW, ROW), :] = slot
        part = jnp.where(lane < 32, face & 255, jnp.where(lane < 64, face >> 8 & 3, face >> 10))
        part = jnp.where(((lane & 31) == (slot & 31)) & (lane < 96), part, 0)
        table = table + jnp.dot(hits[b], part.astype(F32).astype(BF), preferred_element_type=F32)
    ids_send[...] = table

    for load in small[2:]:
        load.wait()
    wgap_v[...] = jnp.zeros_like(wgap_v)
    wgap_v[NODES:, 0:NODES] = d_ref[...]
    wgap_v[NODES:, ROW : ROW + NODES] = -m_ref[...]
    mtwo = jnp.concatenate([m_ref[...], m_ref[...]], axis=1)
    mfour_v[...] = jnp.zeros_like(mfour_v)
    mfour_v[NODES:, 0:ROW] = mtwo
    mfour_v[NODES:, ROW:] = mtwo
    for half in range(2):
        pick = jnp.where((down == lane + half * NODES) & (lane < NODES), 0.5, 0.0)
        wcond_v[half, 0:ROW, :] = pick.astype(BF)
        wcond_v[half, ROW:, :] = (conduct_ref[...].astype(F32) * -0.5).astype(BF)
    wide_d, wide_l = iota((ROW, SLOTS), 0), iota((ROW, SLOTS), 1)
    tile = jnp.where(wide_d == (wide_l & 31), 1.0, jnp.where(wide_d == (wide_l & 31) + 64, 256.0, 0.0))
    tile_v[...] = tile.astype(BF)
    down2, lane2 = iota((ROW, 2 * ROW), 0), iota((ROW, 2 * ROW), 1)
    part2 = down2 >> 5
    spread = jnp.where(
        lane2 < ROW,
        jnp.where(part2 == 0, 1.0, jnp.where(part2 == 1, 256.0, 0.0)),
        jnp.where(part2 == 1, 1.0, jnp.where(part2 == 2, 4.0, 0.0)),
    )
    spread_v[...] = spread.astype(BF)
    totals_v[...] = jnp.zeros_like(totals_v)
    acc_v[...] = jnp.zeros_like(acc_v)

    loads[0].wait()

    def pack(g, _):
        want = iota((SLOTS, ROW), 0) + g * SLOTS
        want = want.astype(F32)
        pick = jnp.concatenate(
            [(want == row8_v[b : b + 1, :]).astype(F32).astype(BF) for b in range(8)], axis=1
        )
        rows = jnp.dot(pick, casting_v[...], preferred_element_type=F32).astype(BF)
        send_v[pl.ds(g * BATCH, BATCH)] = rows.reshape(BATCH, PER, ROW)
        return 0

    lax.fori_loop(0, BATCHES, pack, 0)
    pl.semaphore_wait(barrier, PEERS - 1)

    def send(g, _):
        def one(g, i):
            j = g * BATCH + i
            to = peer(g, i, 1)
            pltpu.make_async_remote_copy(
                src_ref=ids_send.at[pl.ds(j, 1)],
                dst_ref=ids_recv.at[pl.ds(j, 1)],
                send_sem=sent_sem.at[0],
                recv_sem=id_sem.at[g],
                device_id=to,
                device_id_type=MESH,
            ).start()
            pltpu.make_async_remote_copy(
                src_ref=send_v.at[j],
                dst_ref=recv_v.at[j],
                send_sem=sent_sem.at[1],
                recv_sem=row_sem.at[g],
                device_id=to,
                device_id_type=MESH,
            ).start()

        def own():
            pltpu.make_async_copy(ids_send.at[pl.ds(0, 1)], ids_recv.at[pl.ds(0, 1)], id_sem.at[0]).start()
            pltpu.make_async_copy(send_v.at[0], recv_v.at[0], row_sem.at[0]).start()

        each_peer(g, one, own)
        return 0

    lax.fori_loop(0, BATCHES, send, 0)
    loads[1].wait()
    loads[2].wait()

    def wait_for(ref, sem):
        pltpu.make_async_copy(ref, ref, sem).wait()

    def settle(g, _):
        span = pl.ds(pl.multiple_of(g * BATCH, BATCH), BATCH)
        wait_for(ids_recv.at[span], id_sem.at[g])
        wait_for(recv_v.at[span], row_sem.at[g])
        ids = ids_recv[span, :]
        across = jnp.dot(ids.astype(BF), tile_v[...], preferred_element_type=F32)
        mine = iota((BATCH, SLOTS), 0) == iota((BATCH, SLOTS), 1) >> 5
        across = jnp.sum(jnp.where(mine, across, 0.0), axis=0, keepdims=True)
        keep = iota((PER, ROW), 0) == (iota((PER, ROW), 1) & 31)
        spaced = jnp.where(keep[None], jnp.broadcast_to(ids[:, None, :], (BATCH, PER, ROW)), 0.0)
        spaced = spaced.reshape(SLOTS, ROW).astype(BF)
        both = jnp.dot(spaced, spread_v[...], preferred_element_type=F32)
        low, high = both[:, :ROW], both[:, ROW:]
        lanes = iota((SLOTS, ROW), 1).astype(F32)
        pick = jnp.concatenate([(low - t * ROW == lanes).astype(F32).astype(BF) for t in range(8)], axis=1)
        found = jnp.dot(pick, mold_v[...], preferred_element_type=F32)
        upper = high >= 4.0
        faces = jnp.where(upper, found[:, ROW:], found[:, :ROW]).astype(BF)
        rows = recv_v[span].reshape(SLOTS, ROW)
        pair = jnp.concatenate([rows, faces], axis=1)
        gap = lax.dot_general(pair, wgap_v[...], (((1,), (1,)), ((), ())), preferred_element_type=F32)
        flux = (rows.astype(F32) * faces.astype(F32) * gap).astype(BF)
        back = jnp.dot(flux, wgap_v[:, :ROW], preferred_element_type=F32)
        answer = (back + gap).astype(BF)
        ans_v[span] = answer.reshape(BATCH, PER, ROW)

        def one(g, i):
            j = g * BATCH + i
            pltpu.make_async_remote_copy(
                src_ref=ans_v.at[j],
                dst_ref=back_v.at[j],
                send_sem=sent_sem.at[2],
                recv_sem=ans_sem.at[g],
                device_id=peer(g, i, -1),
                device_id_type=MESH,
            ).start()

        def own():
            pltpu.make_async_copy(ans_v.at[0], back_v.at[0], ans_sem.at[0]).start()

        each_peer(g, one, own)
        gain = jnp.dot(flux, mfour_v[...], preferred_element_type=F32)
        column = jnp.where(upper, high - 4.0, high)
        block = (iota((SLOTS, ROW), 1) >> 6).astype(F32)
        gain = jnp.concatenate(
            [
                jnp.where(column == block, gain[:, :ROW], 0.0).astype(BF),
                jnp.where(column == block + 2.0, gain[:, ROW:], 0.0).astype(BF),
            ],
            axis=1,
        )
        put = (iota((SLOTS, SLOTS), 0).astype(F32) == across).astype(F32).astype(BF)
        totals_v[...] += jnp.dot(put, gain, preferred_element_type=F32)
        return 0

    lax.fori_loop(0, BATCHES, settle, 0)

    for q in range(4):
        rows = slice((q // 2) * 256, (q // 2) * 256 + 256)
        cols = slice((q % 2) * ROW, (q % 2) * ROW + ROW)
        quarter_v[q] = totals_v[rows, cols].astype(BF)
    for d in range(4):
        v = lax.rem(x + d, 4)
        if d == 0:
            pltpu.make_async_copy(quarter_v.at[v], placed_v.at[x], tot_sem.at[0]).start()
        else:
            pltpu.make_async_remote_copy(
                src_ref=quarter_v.at[v],
                dst_ref=placed_v.at[x],
                send_sem=sent_sem.at[3],
                recv_sem=tot_sem.at[0],
                device_id=(surf, v),
                device_id_type=MESH,
            ).start()

    def collect(g, _):
        span = pl.ds(pl.multiple_of(g * BATCH, BATCH), BATCH)
        wait_for(back_v.at[span], ans_sem.at[g])
        lanes = iota((SEGS, ROW), 1) + g * SLOTS
        slots = slotrep_v[...]
        pick = jnp.concatenate(
            [(slots == lanes + t * ROW).astype(F32).astype(BF) for t in range(SLOTS // ROW)], axis=1
        )
        acc_v[...] += jnp.dot(pick, back_v[span].reshape(SLOTS, ROW), preferred_element_type=F32)
        return 0

    lax.fori_loop(0, BATCHES - 2, collect, 0)

    loads[3].wait()
    wait_for(placed_v, tot_sem.at[0])
    for u in range(4):
        for half in range(2):
            rows = slice(u * QUARTER + half * 256, u * QUARTER + half * 256 + 256)
            volume = volume_v[rows, :]
            both = jnp.concatenate([placed_v[u], volume], axis=1)
            change = jnp.dot(both, wcond_v[half], preferred_element_type=F32)
            mout_v[rows, :] = (volume.astype(F32) + change).astype(BF)
    mold_store = pltpu.make_async_copy(mout_v, mout_hbm, out_sem.at[0])
    mold_store.start()

    lax.fori_loop(BATCHES - 2, BATCHES, collect, 0)
    cout_v[...] = acc_v[...].astype(BF)
    casting_store = pltpu.make_async_copy(cout_v, cout_hbm, out_sem.at[1])
    casting_store.start()
    wait_for(ids_send.at[pl.ds(1, PEERS - 1)], sent_sem.at[0])
    wait_for(send_v.at[pl.ds(1, PEERS - 1)], sent_sem.at[1])
    wait_for(ans_v.at[pl.ds(1, PEERS - 1)], sent_sem.at[2])
    wait_for(quarter_v.at[pl.ds(0, 3)], sent_sem.at[3])
    mold_store.wait()
    casting_store.wait()


def local(casting, owner, face_id, mold_faces, mortar_d, mortar_m, conduct, volume):
    hbm = pl.BlockSpec(memory_space=pltpu.HBM)
    slots = (PEERS, PER, ROW)
    return pl.pallas_call(
        kernel,
        out_shape=(
            jax.ShapeDtypeStruct((SEGS, ROW), BF),
            jax.ShapeDtypeStruct((FACES, ROW), BF),
        ),
        in_specs=[hbm] * 8,
        out_specs=(hbm, hbm),
        scratch_shapes=[
            pltpu.VMEM((8, ROW), I32),
            pltpu.VMEM((8, ROW), I32),
            pltpu.VMEM((NODES, NODES), BF),
            pltpu.VMEM((NODES, NODES), BF),
            pltpu.VMEM((ROW, ROW), BF),
            pltpu.VMEM((SEGS, ROW), BF),
            pltpu.VMEM((1024, 2 * ROW), BF),
            pltpu.VMEM((FACES, ROW), BF),
            pltpu.VMEM(slots, BF),
            pltpu.VMEM(slots, BF),
            pltpu.VMEM(slots, BF),
            pltpu.VMEM(slots, BF),
            pltpu.VMEM((PEERS, ROW), F32),
            pltpu.VMEM((PEERS, ROW), F32),
            pltpu.VMEM((ROW, 2 * ROW), BF),
            pltpu.VMEM((ROW, 2 * ROW), BF),
            pltpu.VMEM((2, 2 * ROW, ROW), BF),
            pltpu.VMEM((ROW, SLOTS), BF),
            pltpu.VMEM((ROW, 2 * ROW), BF),
            pltpu.VMEM((8, ROW), F32),
            pltpu.VMEM((SEGS, ROW), I32),
            pltpu.VMEM((SLOTS, 2 * ROW), F32),
            pltpu.VMEM((4, 256, ROW), BF),
            pltpu.VMEM((4, 256, ROW), BF),
            pltpu.VMEM((SEGS, ROW), F32),
            pltpu.VMEM((SEGS, ROW), BF),
            pltpu.VMEM((FACES, ROW), BF),
            pltpu.SemaphoreType.DMA((9,)),
            pltpu.SemaphoreType.DMA((2,)),
            pltpu.SemaphoreType.DMA((BATCHES,)),
            pltpu.SemaphoreType.DMA((BATCHES,)),
            pltpu.SemaphoreType.DMA((BATCHES,)),
            pltpu.SemaphoreType.DMA((1,)),
            pltpu.SemaphoreType.DMA((4,)),
        ],
        compiler_params=pltpu.CompilerParams(
            collective_id=0, has_side_effects=True, vmem_limit_bytes=60 * 2**20
        ),
        cost_estimate=pl.CostEstimate(
            flops=2 * 4096 * 1024 * 1024, bytes_accessed=2 * 2**20, transcendentals=0
        ),
    )(
        owner.reshape(8, ROW),
        face_id.reshape(8, ROW),
        mortar_d,
        mortar_m,
        conduct,
        casting,
        mold_faces,
        volume,
    )


def solution(mesh):
    rows, flat = P(("surf", "vol"), None), P(("surf", "vol"))
    return jax.shard_map(
        local,
        mesh=mesh,
        in_specs=(rows, rows, flat, rows, P(), P(), P(), rows),
        out_specs=(rows, rows),
        check_vma=False,
    )
```

```python
import functools

import jax
import jax.numpy as jnp
from jax import lax
from jax.experimental import pallas as pl
from jax.experimental.pallas import tpu as pltpu
from jax.sharding import PartitionSpec as P

MESH = pl.DeviceIdType.MESH
BF = jnp.bfloat16
F32 = jnp.float32
I32 = jnp.int32

PEERS = 128
PER = 32
BATCH = 16
BATCHES = PEERS // BATCH
SLOTS = BATCH * PER
NODES = 64
ROW = 128
SEGS = 1024
FACES = 2048
QUARTER = FACES // 4


def iota(shape, dim):
    return lax.broadcasted_iota(I32, shape, dim)


def kernel(
    owner_hbm,
    face_hbm,
    d_hbm,
    m_hbm,
    conduct_hbm,
    casting_hbm,
    mold_hbm,
    volume_hbm,
    cout_v,
    mout_v,
    owner_ref,
    face_ref,
    d_ref,
    m_ref,
    conduct_ref,
    casting_v,
    mold_v,
    volume_v,
    send_v,
    recv_v,
    ans_v,
    back_v,
    ids_send,
    ids_recv,
    wgap_v,
    mfour_v,
    wcond_v,
    tile_v,
    spread_v,
    row8_v,
    slotrep_v,
    totals_v,
    quarter_v,
    placed_v,
    acc_v,
    load_sem,
    row_sem,
    id_sem,
    ans_sem,
    tot_sem,
    sent_sem,
):
    surf = lax.axis_index("surf")
    x = lax.axis_index("vol")
    z, y, c = surf // 8, lax.rem(surf // 2, 4), lax.rem(surf, 2)

    along_z = {n: [lax.rem(z + 4 + n * d, 4) * 8 for d in range(4)] for n in (1, -1)}
    along_y = {n: [lax.rem(y + 4 + n * d, 4) * 2 for d in range(4)] for n in (1, -1)}

    def peers(g, sign):
        along_x = [lax.rem(x + 16 + sign * (g // 2 + d), 4) for d in range(4)]
        core = [lax.rem(c + g + d, 2) for d in range(2)]
        found = []
        for i in range(BATCH):
            dz, dy = i // 4, i % 4
            found.append((along_z[sign][dz] + along_y[sign][dy] + core[dz % 2], along_x[(dz + dy) % 4]))
        return found

    def each_peer(g, sign, act, own):
        found = peers(g, sign)
        for i in range(BATCH):
            if i > 0:
                act(g * BATCH + i, found[i])
            elif isinstance(g, int):
                if g > 0:
                    act(g * BATCH, found[0])
                elif own is not None:
                    own()
            else:
                pl.when(g > 0)(functools.partial(act, g * BATCH, found[0]))
                if own is not None:
                    pl.when(g == 0)(own)

    small = [
        pltpu.make_async_copy(source, place, load_sem.at[4 + n])
        for n, (source, place) in enumerate(
            [
                (owner_hbm, owner_ref),
                (face_hbm, face_ref),
                (d_hbm, d_ref),
                (m_hbm, m_ref),
                (conduct_hbm, conduct_ref),
            ]
        )
    ]
    loads = [
        pltpu.make_async_copy(casting_hbm, casting_v, load_sem.at[0]),
        pltpu.make_async_copy(mold_hbm.at[pl.ds(0, 1024)], mold_v.at[:, pl.ds(0, ROW)], load_sem.at[1]),
        pltpu.make_async_copy(mold_hbm.at[pl.ds(1024, 1024)], mold_v.at[:, pl.ds(ROW, ROW)], load_sem.at[2]),
        pltpu.make_async_copy(volume_hbm, volume_v, load_sem.at[3]),
    ]
    for load in small + loads:
        load.start()

    barrier = pltpu.get_barrier_semaphore()

    def greet(_, to):
        pl.semaphore_signal(barrier, inc=1, device_id=to, device_id_type=MESH)

    for g in range(BATCHES):
        each_peer(g, 1, greet, None)

    small[0].wait()
    owner = owner_ref[...]
    dx = (owner & 3) - x & 3
    dc = (owner >> 2 & 1) - c & 1
    dy = (owner >> 3 & 3) - y & 3
    dz = (owner >> 5 & 3) - z & 3
    order = (dx - dz - dy & 3) * 32 + (dc - dz & 1) * 16 + dz * 4 + dy
    down, lane = iota((ROW, ROW), 0), iota((ROW, ROW), 1)
    before = jnp.concatenate([(down < lane).astype(F32), jnp.ones((ROW, ROW), F32)], axis=1).astype(BF)
    hits, sofar = [], jnp.zeros((PEERS, ROW), F32)
    for b in range(8):
        hit = down == order[b : b + 1, :]
        hits.append(hit.astype(F32).astype(BF))
        count = jnp.dot(hits[b], before, preferred_element_type=F32)
        rank = jnp.sum(jnp.where(hit, count[:, :ROW] + sofar, 0.0), axis=0, keepdims=True)
        sofar = sofar + count[:, ROW:]
        row8_v[b : b + 1, :] = rank
    slot8 = (order * PER).astype(F32) + row8_v[...]
    row8_v[...] = slot8
    slot_t = slot8.T
    small[1].wait()
    face_t = face_ref[...].astype(F32).T
    table = jnp.zeros((PEERS, ROW), F32)
    for b in range(8):
        slot = jnp.broadcast_to(slot_t[:, b : b + 1], (ROW, ROW)).astype(I32)
        face = jnp.broadcast_to(face_t[:, b : b + 1], (ROW, ROW)).astype(I32)
        slotrep_v[pl.ds(b * ROW, ROW), :] = slot
        part = jnp.where(lane < 32, face & 255, jnp.where(lane < 64, face >> 8 & 3, face >> 10))
        part = jnp.where(((lane & 31) == (slot & 31)) & (lane < 96), part, 0)
        table = table + jnp.dot(hits[b], part.astype(F32).astype(BF), preferred_element_type=F32)
    ids_send[...] = table

    loads[0].wait()

    def pack(g, _):
        want = iota((SLOTS, ROW), 0) + g * SLOTS
        want = want.astype(F32)
        pick = jnp.concatenate(
            [(want == row8_v[b : b + 1, :]).astype(F32).astype(BF) for b in range(8)], axis=1
        )
        rows = jnp.dot(pick, casting_v[...], preferred_element_type=F32).astype(BF)
        send_v[pl.ds(g * BATCH, BATCH)] = rows.reshape(BATCH, PER, ROW)
        return 0

    pack(0, 0)
    pack(1, 0)
    pl.semaphore_wait(barrier, PEERS - 1)

    def send(g, _):
        def one(j, to):
            pltpu.make_async_remote_copy(
                src_ref=ids_send.at[pl.ds(j, 1)],
                dst_ref=ids_recv.at[pl.ds(j, 1)],
                send_sem=sent_sem.at[0],
                recv_sem=id_sem.at[g],
                device_id=to,
                device_id_type=MESH,
            ).start()
            pltpu.make_async_remote_copy(
                src_ref=send_v.at[j],
                dst_ref=recv_v.at[j],
                send_sem=sent_sem.at[1],
                recv_sem=row_sem.at[g],
                device_id=to,
                device_id_type=MESH,
            ).start()

        def own():
            pltpu.make_async_copy(ids_send.at[pl.ds(0, 1)], ids_recv.at[pl.ds(0, 1)], id_sem.at[0]).start()
            pltpu.make_async_copy(send_v.at[0], recv_v.at[0], row_sem.at[0]).start()

        each_peer(g, 1, one, own)

        @pl.when(g < BATCHES - 2)
        def _():
            pack(g + 2, 0)

        return 0

    lax.fori_loop(0, BATCHES, send, 0)

    for load in small[2:]:
        load.wait()
    wgap_v[...] = jnp.zeros_like(wgap_v)
    wgap_v[NODES:, 0:NODES] = d_ref[...]
    wgap_v[NODES:, ROW : ROW + NODES] = -m_ref[...]
    mtwo = jnp.concatenate([m_ref[...], m_ref[...]], axis=1)
    mfour_v[...] = jnp.zeros_like(mfour_v)
    mfour_v[NODES:, 0:ROW] = mtwo
    mfour_v[NODES:, ROW:] = mtwo
    for half in range(2):
        pick = jnp.where((down == lane + half * NODES) & (lane < NODES), 0.5, 0.0)
        wcond_v[half, 0:ROW, :] = pick.astype(BF)
        wcond_v[half, ROW:, :] = (conduct_ref[...].astype(F32) * -0.5).astype(BF)
    wide_d, wide_l = iota((ROW, SLOTS), 0), iota((ROW, SLOTS), 1)
    tile = jnp.where(wide_d == (wide_l & 31), 1.0, jnp.where(wide_d == (wide_l & 31) + 64, 256.0, 0.0))
    tile_v[...] = tile.astype(BF)
    down2, lane2 = iota((ROW, 2 * ROW), 0), iota((ROW, 2 * ROW), 1)
    part2 = down2 >> 5
    spread = jnp.where(
        lane2 < ROW,
        jnp.where(part2 == 0, 1.0, jnp.where(part2 == 1, 256.0, 0.0)),
        jnp.where(part2 == 1, 1.0, jnp.where(part2 == 2, 4.0, 0.0)),
    )
    spread_v[...] = spread.astype(BF)
    totals_v[...] = jnp.zeros_like(totals_v)
    acc_v[...] = jnp.zeros_like(acc_v)

    loads[1].wait()
    loads[2].wait()

    def wait_for(ref, sem):
        pltpu.make_async_copy(ref, ref, sem).wait()

    def settle(g, _):
        span = pl.ds(pl.multiple_of(g * BATCH, BATCH), BATCH)
        wait_for(ids_recv.at[span], id_sem.at[g])
        wait_for(recv_v.at[span], row_sem.at[g])
        ids = ids_recv[span, :]
        across = jnp.dot(ids.astype(BF), tile_v[...], preferred_element_type=F32)
        mine = iota((BATCH, SLOTS), 0) == iota((BATCH, SLOTS), 1) >> 5
        across = jnp.sum(jnp.where(mine, across, 0.0), axis=0, keepdims=True)
        keep = iota((PER, ROW), 0) == (iota((PER, ROW), 1) & 31)
        spaced = jnp.where(keep[None], jnp.broadcast_to(ids[:, None, :], (BATCH, PER, ROW)), 0.0)
        spaced = spaced.reshape(SLOTS, ROW).astype(BF)
        both = jnp.dot(spaced, spread_v[...], preferred_element_type=F32)
        low, high = both[:, :ROW], both[:, ROW:]
        lanes = iota((SLOTS, ROW), 1).astype(F32)
        pick = jnp.concatenate([(low - t * ROW == lanes).astype(F32).astype(BF) for t in range(8)], axis=1)
        found = jnp.dot(pick, mold_v[...], preferred_element_type=F32)
        upper = high >= 4.0
        faces = jnp.where(upper, found[:, ROW:], found[:, :ROW]).astype(BF)
        rows = recv_v[span].reshape(SLOTS, ROW)
        pair = jnp.concatenate([rows, faces], axis=1)
        gap = lax.dot_general(pair, wgap_v[...], (((1,), (1,)), ((), ())), preferred_element_type=F32)
        flux = (rows.astype(F32) * faces.astype(F32) * gap).astype(BF)
        back = jnp.dot(flux, wgap_v[:, :ROW], preferred_element_type=F32)
        answer = (back + gap).astype(BF)
        ans_v[span] = answer.reshape(BATCH, PER, ROW)

        def one(j, to):
            pltpu.make_async_remote_copy(
                src_ref=ans_v.at[j],
                dst_ref=back_v.at[j],
                send_sem=sent_sem.at[2],
                recv_sem=ans_sem.at[g],
                device_id=to,
                device_id_type=MESH,
            ).start()

        def own():
            pltpu.make_async_copy(ans_v.at[0], back_v.at[0], ans_sem.at[0]).start()

        each_peer(g, -1, one, own)
        gain = jnp.dot(flux, mfour_v[...], preferred_element_type=F32)
        column = jnp.where(upper, high - 4.0, high)
        block = (iota((SLOTS, ROW), 1) >> 6).astype(F32)
        gain = jnp.concatenate(
            [
                jnp.where(column == block, gain[:, :ROW], 0.0).astype(BF),
                jnp.where(column == block + 2.0, gain[:, ROW:], 0.0).astype(BF),
            ],
            axis=1,
        )
        put = (iota((SLOTS, SLOTS), 0).astype(F32) == across).astype(F32).astype(BF)
        totals_v[...] += jnp.dot(put, gain, preferred_element_type=F32)
        return 0

    lax.fori_loop(0, BATCHES, settle, 0)

    for q in range(4):
        rows = slice((q // 2) * 256, (q // 2) * 256 + 256)
        cols = slice((q % 2) * ROW, (q % 2) * ROW + ROW)
        quarter_v[q] = totals_v[rows, cols].astype(BF)
    for d in range(4):
        v = lax.rem(x + d, 4)
        if d == 0:
            pltpu.make_async_copy(quarter_v.at[v], placed_v.at[x], tot_sem.at[0]).start()
        else:
            pltpu.make_async_remote_copy(
                src_ref=quarter_v.at[v],
                dst_ref=placed_v.at[x],
                send_sem=sent_sem.at[3],
                recv_sem=tot_sem.at[0],
                device_id=(surf, v),
                device_id_type=MESH,
            ).start()

    def collect(g, _):
        span = pl.ds(pl.multiple_of(g * BATCH, BATCH), BATCH)
        wait_for(back_v.at[span], ans_sem.at[g])
        lanes = iota((SEGS, ROW), 1) + g * SLOTS
        slots = slotrep_v[...]
        pick = jnp.concatenate(
            [(slots == lanes + t * ROW).astype(F32).astype(BF) for t in range(SLOTS // ROW)], axis=1
        )
        acc_v[...] += jnp.dot(pick, back_v[span].reshape(SLOTS, ROW), preferred_element_type=F32)
        return 0

    lax.fori_loop(0, BATCHES - 2, collect, 0)

    loads[3].wait()
    wait_for(placed_v, tot_sem.at[0])
    for u in range(4):
        for half in range(2):
            rows = slice(u * QUARTER + half * 256, u * QUARTER + half * 256 + 256)
            volume = volume_v[rows, :]
            both = jnp.concatenate([placed_v[u], volume], axis=1)
            change = jnp.dot(both, wcond_v[half], preferred_element_type=F32)
            mout_v[rows, :] = (volume.astype(F32) + change).astype(BF)

    lax.fori_loop(BATCHES - 2, BATCHES, collect, 0)
    cout_v[...] = acc_v[...].astype(BF)
    wait_for(ids_send.at[pl.ds(1, PEERS - 1)], sent_sem.at[0])
    wait_for(send_v.at[pl.ds(1, PEERS - 1)], sent_sem.at[1])
    wait_for(ans_v.at[pl.ds(1, PEERS - 1)], sent_sem.at[2])
    wait_for(quarter_v.at[pl.ds(0, 3)], sent_sem.at[3])


def local(casting, owner, face_id, mold_faces, mortar_d, mortar_m, conduct, volume):
    hbm = pl.BlockSpec(memory_space=pltpu.HBM)
    vmem = pl.BlockSpec(memory_space=pltpu.VMEM)
    slots = (PEERS, PER, ROW)
    return pl.pallas_call(
        kernel,
        out_shape=(
            jax.ShapeDtypeStruct((SEGS, ROW), BF),
            jax.ShapeDtypeStruct((FACES, ROW), BF),
        ),
        in_specs=[hbm] * 8,
        out_specs=(vmem, vmem),
        scratch_shapes=[
            pltpu.VMEM((8, ROW), I32),
            pltpu.VMEM((8, ROW), I32),
            pltpu.VMEM((NODES, NODES), BF),
            pltpu.VMEM((NODES, NODES), BF),
            pltpu.VMEM((ROW, ROW), BF),
            pltpu.VMEM((SEGS, ROW), BF),
            pltpu.VMEM((1024, 2 * ROW), BF),
            pltpu.VMEM((FACES, ROW), BF),
            pltpu.VMEM(slots, BF),
            pltpu.VMEM(slots, BF),
            pltpu.VMEM(slots, BF),
            pltpu.VMEM(slots, BF),
            pltpu.VMEM((PEERS, ROW), F32),
            pltpu.VMEM((PEERS, ROW), F32),
            pltpu.VMEM((ROW, 2 * ROW), BF),
            pltpu.VMEM((ROW, 2 * ROW), BF),
            pltpu.VMEM((2, 2 * ROW, ROW), BF),
            pltpu.VMEM((ROW, SLOTS), BF),
            pltpu.VMEM((ROW, 2 * ROW), BF),
            pltpu.VMEM((8, ROW), F32),
            pltpu.VMEM((SEGS, ROW), I32),
            pltpu.VMEM((SLOTS, 2 * ROW), F32),
            pltpu.VMEM((4, 256, ROW), BF),
            pltpu.VMEM((4, 256, ROW), BF),
            pltpu.VMEM((SEGS, ROW), F32),
            pltpu.SemaphoreType.DMA((9,)),
            pltpu.SemaphoreType.DMA((BATCHES,)),
            pltpu.SemaphoreType.DMA((BATCHES,)),
            pltpu.SemaphoreType.DMA((BATCHES,)),
            pltpu.SemaphoreType.DMA((1,)),
            pltpu.SemaphoreType.DMA((4,)),
        ],
        compiler_params=pltpu.CompilerParams(
            collective_id=0, has_side_effects=True, vmem_limit_bytes=40 * 2**20
        ),
        cost_estimate=pl.CostEstimate(
            flops=2 * 4096 * 1024 * 1024, bytes_accessed=2 * 2**20, transcendentals=0
        ),
    )(
        *(
            pltpu.with_memory_space_constraint(a, pltpu.HBM)
            for a in (
                owner.reshape(8, ROW),
                face_id.reshape(8, ROW),
                mortar_d,
                mortar_m,
                conduct,
                casting,
                mold_faces,
                volume,
            )
        )
    )


def solution(mesh):
    rows, flat = P(("surf", "vol"), None), P(("surf", "vol"))
    return jax.shard_map(
        local,
        mesh=mesh,
        in_specs=(rows, rows, flat, rows, P(), P(), P(), rows),
        out_specs=(rows, rows),
        check_vma=False,
    )
```

```python
import functools
import itertools

import jax
import jax.numpy as jnp
import numpy as np
from jax import lax
from jax.experimental import pallas as pl
from jax.experimental.pallas import tpu as pltpu
from jax.sharding import PartitionSpec as P

MESH = pl.DeviceIdType.MESH
BF = jnp.bfloat16
F32 = jnp.float32
I32 = jnp.int32

PEERS = 128
PER = 32
BATCH = 16
BATCHES = PEERS // BATCH
SLOTS = BATCH * PER
NODES = 64
ROW = 128
SEGS = 1024
FACES = 2048
QUARTER = FACES // 4


def hops(offset):
    dz, dy, _, dx = offset
    return sum(min(d, 4 - d) for d in (dz, dy, dx))


def in_order():
    offsets = list(itertools.product(range(4), range(4), range(2), range(4)))
    rest = offsets[1:]
    def key(o):
        dz, dy, dc, dx = o
        return ((dx - dz - dy & 3) * 2 + (dc - dz & 1)) * 16 + dz * 4 + dy
    rest.sort(key=key)
    return offsets[:1] + rest


ORDER = in_order()
PLACE = np.zeros((8, 128), np.float32)
for at, (oz, oy, oc, ox) in enumerate(ORDER):
    PLACE[:, ((oz * 4 + oy) * 2 + oc) * 4 + ox] = at
PACKED = [
    [sum(ORDER[g * BATCH + i][n] << 2 * g for g in range(BATCHES)) for i in range(BATCH)]
    for n in range(4)
]


def iota(shape, dim):
    return lax.broadcasted_iota(I32, shape, dim)


def kernel(
    owner_hbm,
    face_hbm,
    place_hbm,
    d_hbm,
    m_hbm,
    conduct_hbm,
    casting_hbm,
    mold_hbm,
    volume_hbm,
    cout_v,
    mout_v,
    owner_ref,
    face_ref,
    place_ref,
    d_ref,
    m_ref,
    conduct_ref,
    casting_v,
    mold_v,
    volume_v,
    send_v,
    recv_v,
    ans_v,
    back_v,
    ids_send,
    ids_recv,
    wgap_v,
    mfour_v,
    wcond_v,
    tile_v,
    spread_v,
    row8_v,
    slotrep_v,
    totals_v,
    quarter_v,
    placed_v,
    acc_v,
    load_sem,
    row_sem,
    id_sem,
    ans_sem,
    tot_sem,
    sent_sem,
):
    surf = lax.axis_index("surf")
    x = lax.axis_index("vol")
    z, y, c = surf // 8, lax.rem(surf // 2, 4), lax.rem(surf, 2)

    def peers(g, sign):
        found = []
        for i in range(BATCH):
            if isinstance(g, int):
                dz, dy, dc, dx = ORDER[g * BATCH + i]
            else:
                dz, dy, dc, dx = (packed[i] >> (2 * g) & 3 for packed in PACKED)
            pz, py, pc, px = z + sign * dz & 3, y + sign * dy & 3, c + dc & 1, x + sign * dx & 3
            found.append((((pz * 8 + py * 2 + pc, px)), ((dz * 4 + dy) * 2 + dc) * 4 + dx))
        return found

    def each_peer(g, sign, act, own):
        found = peers(g, sign)
        for i in range(BATCH):
            if i > 0:
                act(g * BATCH + i, *found[i])
            elif isinstance(g, int):
                if g > 0:
                    act(g * BATCH, *found[0])
            else:
                pl.when(g > 0)(functools.partial(act, g * BATCH, *found[0]))
                if own is not None:
                    pl.when(g == 0)(own)

    small = [
        pltpu.make_async_copy(source, place, load_sem.at[4 + n])
        for n, (source, place) in enumerate(
            [
                (owner_hbm, owner_ref),
                (face_hbm, face_ref),
                (place_hbm, place_ref),
                (d_hbm, d_ref),
                (m_hbm, m_ref),
                (conduct_hbm, conduct_ref),
            ]
        )
    ]
    loads = [
        pltpu.make_async_copy(casting_hbm, casting_v, load_sem.at[0]),
        pltpu.make_async_copy(mold_hbm.at[pl.ds(0, 1024)], mold_v.at[:, pl.ds(0, ROW)], load_sem.at[1]),
        pltpu.make_async_copy(mold_hbm.at[pl.ds(1024, 1024)], mold_v.at[:, pl.ds(ROW, ROW)], load_sem.at[2]),
        pltpu.make_async_copy(volume_hbm, volume_v, load_sem.at[3]),
    ]
    for load in small + loads:
        load.start()

    barrier = pltpu.get_barrier_semaphore()

    far_first = sorted(range(1, PEERS), key=lambda j: -hops(ORDER[j]))
    for j in far_first:
        dz, dy, dc, dx = ORDER[j]
        to = ((z + dz & 3) * 8 + (y + dy & 3) * 2 + (c + dc & 1), x + dx & 3)
        pl.semaphore_signal(barrier, inc=1, device_id=to, device_id_type=MESH)

    small[0].wait()
    owner = owner_ref[...]
    dx = (owner & 3) - x & 3
    dc = (owner >> 2 & 1) - c & 1
    dy = (owner >> 3 & 3) - y & 3
    dz = (owner >> 5 & 3) - z & 3
    offset = ((dz * 4 + dy) * 2 + dc) * 4 + dx
    down, lane = iota((ROW, ROW), 0), iota((ROW, ROW), 1)
    before = jnp.concatenate([(down < lane).astype(F32), jnp.ones((ROW, ROW), F32)], axis=1).astype(BF)
    small[2].wait()
    place = place_ref[...].astype(BF)
    hits, sofar = [], jnp.zeros((PEERS, ROW), F32)
    for b in range(8):
        hit = down == offset[b : b + 1, :]
        hits.append(hit.astype(F32).astype(BF))
        count = jnp.dot(hits[b], before, preferred_element_type=F32)
        rank = jnp.sum(jnp.where(hit, count[:, :ROW] + sofar, 0.0), axis=0, keepdims=True)
        sofar = sofar + count[:, ROW:]
        order = jnp.dot(place, hits[b], preferred_element_type=F32)[0:1]
        row8_v[b : b + 1, :] = order * PER + rank
    slot8 = row8_v[...]
    slot_t = slot8.T
    small[1].wait()
    face_t = face_ref[...].astype(F32).T
    table = jnp.zeros((PEERS, ROW), F32)
    for b in range(8):
        slot = jnp.broadcast_to(slot_t[:, b : b + 1], (ROW, ROW)).astype(I32)
        face = jnp.broadcast_to(face_t[:, b : b + 1], (ROW, ROW)).astype(I32)
        slotrep_v[pl.ds(b * ROW, ROW), :] = slot
        part = jnp.where(lane < 32, face & 255, jnp.where(lane < 64, face >> 8 & 3, face >> 10))
        part = jnp.where(((lane & 31) == (slot & 31)) & (lane < 96), part, 0)
        table = table + jnp.dot(hits[b], part.astype(F32).astype(BF), preferred_element_type=F32)
    ids_send[...] = table

    loads[0].wait()

    def pack(g, _):
        want = iota((SLOTS, ROW), 0) + g * SLOTS
        want = want.astype(F32)
        pick = jnp.concatenate(
            [(want == row8_v[b : b + 1, :]).astype(F32).astype(BF) for b in range(8)], axis=1
        )
        rows = jnp.dot(pick, casting_v[...], preferred_element_type=F32).astype(BF)
        send_v[pl.ds(g * BATCH, BATCH)] = rows.reshape(BATCH, PER, ROW)
        return 0

    pack(0, 0)
    pack(1, 0)
    pl.semaphore_wait(barrier, PEERS - 1)

    def send(g, _):
        def one(j, to, k):
            pltpu.make_async_remote_copy(
                src_ref=ids_send.at[pl.ds(k, 1)],
                dst_ref=ids_recv.at[pl.ds(j, 1)],
                send_sem=sent_sem.at[0],
                recv_sem=id_sem.at[g],
                device_id=to,
                device_id_type=MESH,
            ).start()
            pltpu.make_async_remote_copy(
                src_ref=send_v.at[j],
                dst_ref=recv_v.at[j],
                send_sem=sent_sem.at[1],
                recv_sem=row_sem.at[g],
                device_id=to,
                device_id_type=MESH,
            ).start()

        def own():
            pltpu.make_async_copy(ids_send.at[pl.ds(0, 1)], ids_recv.at[pl.ds(0, 1)], id_sem.at[0]).start()
            pltpu.make_async_copy(send_v.at[0], recv_v.at[0], row_sem.at[0]).start()

        each_peer(g, 1, one, own)

        @pl.when(g < BATCHES - 2)
        def _():
            pack(g + 2, 0)

        return 0

    lax.fori_loop(0, BATCHES, send, 0)

    for load in small[3:]:
        load.wait()
    wgap_v[...] = jnp.zeros_like(wgap_v)
    wgap_v[NODES:, 0:NODES] = d_ref[...]
    wgap_v[NODES:, ROW : ROW + NODES] = -m_ref[...]
    mtwo = jnp.concatenate([m_ref[...], m_ref[...]], axis=1)
    mfour_v[...] = jnp.zeros_like(mfour_v)
    mfour_v[NODES:, 0:ROW] = mtwo
    mfour_v[NODES:, ROW:] = mtwo
    for half in range(2):
        pick = jnp.where((down == lane + half * NODES) & (lane < NODES), 0.5, 0.0)
        wcond_v[half, 0:ROW, :] = pick.astype(BF)
        wcond_v[half, ROW:, :] = (conduct_ref[...].astype(F32) * -0.5).astype(BF)
    wide_d, wide_l = iota((ROW, SLOTS), 0), iota((ROW, SLOTS), 1)
    tile = jnp.where(wide_d == (wide_l & 31), 1.0, jnp.where(wide_d == (wide_l & 31) + 64, 256.0, 0.0))
    tile_v[...] = tile.astype(BF)
    down2, lane2 = iota((ROW, 2 * ROW), 0), iota((ROW, 2 * ROW), 1)
    part2 = down2 >> 5
    spread = jnp.where(
        lane2 < ROW,
        jnp.where(part2 == 0, 1.0, jnp.where(part2 == 1, 256.0, 0.0)),
        jnp.where(part2 == 1, 1.0, jnp.where(part2 == 2, 4.0, 0.0)),
    )
    spread_v[...] = spread.astype(BF)
    totals_v[...] = jnp.zeros_like(totals_v)
    acc_v[...] = jnp.zeros_like(acc_v)

    loads[1].wait()
    loads[2].wait()

    def wait_for(ref, sem):
        pltpu.make_async_copy(ref, ref, sem).wait()

    def settle(g, _):
        span = pl.ds(pl.multiple_of(g * BATCH, BATCH), BATCH)
        wait_for(ids_recv.at[span], id_sem.at[g])
        wait_for(recv_v.at[span], row_sem.at[g])
        ids = ids_recv[span, :]
        across = jnp.dot(ids.astype(BF), tile_v[...], preferred_element_type=F32)
        mine = iota((BATCH, SLOTS), 0) == iota((BATCH, SLOTS), 1) >> 5
        across = jnp.sum(jnp.where(mine, across, 0.0), axis=0, keepdims=True)
        keep = iota((PER, ROW), 0) == (iota((PER, ROW), 1) & 31)
        spaced = jnp.where(keep[None], jnp.broadcast_to(ids[:, None, :], (BATCH, PER, ROW)), 0.0)
        spaced = spaced.reshape(SLOTS, ROW).astype(BF)
        both = jnp.dot(spaced, spread_v[...], preferred_element_type=F32)
        low, high = both[:, :ROW], both[:, ROW:]
        lanes = iota((SLOTS, ROW), 1).astype(F32)
        pick = jnp.concatenate([(low - t * ROW == lanes).astype(F32).astype(BF) for t in range(8)], axis=1)
        found = jnp.dot(pick, mold_v[...], preferred_element_type=F32)
        upper = high >= 4.0
        faces = jnp.where(upper, found[:, ROW:], found[:, :ROW]).astype(BF)
        rows = recv_v[span].reshape(SLOTS, ROW)
        pair = jnp.concatenate([rows, faces], axis=1)
        gap = lax.dot_general(pair, wgap_v[...], (((1,), (1,)), ((), ())), preferred_element_type=F32)
        flux = (rows.astype(F32) * faces.astype(F32) * gap).astype(BF)
        back = jnp.dot(flux, wgap_v[:, :ROW], preferred_element_type=F32)
        answer = (back + gap).astype(BF)
        ans_v[span] = answer.reshape(BATCH, PER, ROW)

        def one(j, to, k):
            pltpu.make_async_remote_copy(
                src_ref=ans_v.at[j],
                dst_ref=back_v.at[j],
                send_sem=sent_sem.at[2],
                recv_sem=ans_sem.at[g],
                device_id=to,
                device_id_type=MESH,
            ).start()

        def own():
            pltpu.make_async_copy(ans_v.at[0], back_v.at[0], ans_sem.at[0]).start()

        each_peer(g, -1, one, own)
        gain = jnp.dot(flux, mfour_v[...], preferred_element_type=F32)
        column = jnp.where(upper, high - 4.0, high)
        block = (iota((SLOTS, ROW), 1) >> 6).astype(F32)
        gain = jnp.concatenate(
            [
                jnp.where(column == block, gain[:, :ROW], 0.0).astype(BF),
                jnp.where(column == block + 2.0, gain[:, ROW:], 0.0).astype(BF),
            ],
            axis=1,
        )
        put = (iota((SLOTS, SLOTS), 0).astype(F32) == across).astype(F32).astype(BF)
        totals_v[...] += jnp.dot(put, gain, preferred_element_type=F32)
        return 0

    lax.fori_loop(0, BATCHES, settle, 0)

    for q in range(4):
        rows = slice((q // 2) * 256, (q // 2) * 256 + 256)
        cols = slice((q % 2) * ROW, (q % 2) * ROW + ROW)
        quarter_v[q] = totals_v[rows, cols].astype(BF)
    for d in range(4):
        v = lax.rem(x + d, 4)
        if d == 0:
            pltpu.make_async_copy(quarter_v.at[v], placed_v.at[x], tot_sem.at[0]).start()
        else:
            pltpu.make_async_remote_copy(
                src_ref=quarter_v.at[v],
                dst_ref=placed_v.at[x],
                send_sem=sent_sem.at[3],
                recv_sem=tot_sem.at[0],
                device_id=(surf, v),
                device_id_type=MESH,
            ).start()

    def collect(g, _):
        span = pl.ds(pl.multiple_of(g * BATCH, BATCH), BATCH)
        wait_for(back_v.at[span], ans_sem.at[g])
        lanes = iota((SEGS, ROW), 1) + g * SLOTS
        slots = slotrep_v[...]
        pick = jnp.concatenate(
            [(slots == lanes + t * ROW).astype(F32).astype(BF) for t in range(SLOTS // ROW)], axis=1
        )
        acc_v[...] += jnp.dot(pick, back_v[span].reshape(SLOTS, ROW), preferred_element_type=F32)
        return 0

    lax.fori_loop(0, BATCHES - 2, collect, 0)

    loads[3].wait()
    wait_for(placed_v, tot_sem.at[0])
    for u in range(4):
        for half in range(2):
            rows = slice(u * QUARTER + half * 256, u * QUARTER + half * 256 + 256)
            volume = volume_v[rows, :]
            both = jnp.concatenate([placed_v[u], volume], axis=1)
            change = jnp.dot(both, wcond_v[half], preferred_element_type=F32)
            mout_v[rows, :] = (volume.astype(F32) + change).astype(BF)

    lax.fori_loop(BATCHES - 2, BATCHES, collect, 0)
    cout_v[...] = acc_v[...].astype(BF)
    wait_for(ids_send.at[pl.ds(1, PEERS - 1)], sent_sem.at[0])
    wait_for(send_v.at[pl.ds(1, PEERS - 1)], sent_sem.at[1])
    wait_for(ans_v.at[pl.ds(1, PEERS - 1)], sent_sem.at[2])
    wait_for(quarter_v.at[pl.ds(0, 3)], sent_sem.at[3])


def store(cast_in, mold_in, cast_out, mold_out, sem):
    copies = [
        pltpu.make_async_copy(cast_in, cast_out, sem.at[0]),
        pltpu.make_async_copy(mold_in, mold_out, sem.at[1]),
    ]
    for copy in copies:
        copy.start()
    for copy in copies:
        copy.wait()


def local(casting, owner, face_id, mold_faces, mortar_d, mortar_m, conduct, volume):
    hbm = pl.BlockSpec(memory_space=pltpu.HBM)
    vmem = pl.BlockSpec(memory_space=pltpu.VMEM)
    slots = (PEERS, PER, ROW)
    made = pl.pallas_call(
        kernel,
        out_shape=(
            jax.ShapeDtypeStruct((SEGS, ROW), BF),
            jax.ShapeDtypeStruct((FACES, ROW), BF),
        ),
        in_specs=[hbm] * 9,
        out_specs=(vmem, vmem),
        scratch_shapes=[
            pltpu.VMEM((8, ROW), I32),
            pltpu.VMEM((8, ROW), I32),
            pltpu.VMEM((8, ROW), F32),
            pltpu.VMEM((NODES, NODES), BF),
            pltpu.VMEM((NODES, NODES), BF),
            pltpu.VMEM((ROW, ROW), BF),
            pltpu.VMEM((SEGS, ROW), BF),
            pltpu.VMEM((1024, 2 * ROW), BF),
            pltpu.VMEM((FACES, ROW), BF),
            pltpu.VMEM(slots, BF),
            pltpu.VMEM(slots, BF),
            pltpu.VMEM(slots, BF),
            pltpu.VMEM(slots, BF),
            pltpu.VMEM((PEERS, ROW), F32),
            pltpu.VMEM((PEERS, ROW), F32),
            pltpu.VMEM((ROW, 2 * ROW), BF),
            pltpu.VMEM((ROW, 2 * ROW), BF),
            pltpu.VMEM((2, 2 * ROW, ROW), BF),
            pltpu.VMEM((ROW, SLOTS), BF),
            pltpu.VMEM((ROW, 2 * ROW), BF),
            pltpu.VMEM((8, ROW), F32),
            pltpu.VMEM((SEGS, ROW), I32),
            pltpu.VMEM((SLOTS, 2 * ROW), F32),
            pltpu.VMEM((4, 256, ROW), BF),
            pltpu.VMEM((4, 256, ROW), BF),
            pltpu.VMEM((SEGS, ROW), F32),
            pltpu.SemaphoreType.DMA((10,)),
            pltpu.SemaphoreType.DMA((BATCHES,)),
            pltpu.SemaphoreType.DMA((BATCHES,)),
            pltpu.SemaphoreType.DMA((BATCHES,)),
            pltpu.SemaphoreType.DMA((1,)),
            pltpu.SemaphoreType.DMA((4,)),
        ],
        compiler_params=pltpu.CompilerParams(
            collective_id=0, has_side_effects=True, vmem_limit_bytes=40 * 2**20
        ),
        cost_estimate=pl.CostEstimate(
            flops=2 * 4096 * 1024 * 1024, bytes_accessed=2 * 2**20, transcendentals=0
        ),
    )(
        *(
            pltpu.with_memory_space_constraint(a, pltpu.HBM)
            for a in (
                owner.reshape(8, ROW),
                face_id.reshape(8, ROW),
                jnp.asarray(PLACE),
                mortar_d,
                mortar_m,
                conduct,
                casting,
                mold_faces,
                volume,
            )
        )
    )
    return pl.pallas_call(
        store,
        out_shape=(
            jax.ShapeDtypeStruct((SEGS, ROW), BF),
            jax.ShapeDtypeStruct((FACES, ROW), BF),
        ),
        in_specs=[vmem] * 2,
        out_specs=(hbm, hbm),
        scratch_shapes=[pltpu.SemaphoreType.DMA((2,))],
    )(*(pltpu.with_memory_space_constraint(a, pltpu.VMEM) for a in made))


def solution(mesh):
    rows, flat = P(("surf", "vol"), None), P(("surf", "vol"))
    return jax.shard_map(
        local,
        mesh=mesh,
        in_specs=(rows, rows, flat, rows, P(), P(), P(), rows),
        out_specs=(rows, rows),
        check_vma=False,
    )
```

```python
import functools
import itertools

import jax
import jax.numpy as jnp
import numpy as np
from jax import lax
from jax.experimental import pallas as pl
from jax.experimental.pallas import tpu as pltpu
from jax.sharding import PartitionSpec as P

MESH = pl.DeviceIdType.MESH
BF = jnp.bfloat16
F32 = jnp.float32
I32 = jnp.int32

PEERS = 128
PER = 32
BATCH = 16
BATCHES = PEERS // BATCH
SLOTS = BATCH * PER
NODES = 64
ROW = 128
SEGS = 1024
FACES = 2048
QUARTER = FACES // 4


def hops(offset):
    dz, dy, _, dx = offset
    return sum(min(d, 4 - d) for d in (dz, dy, dx))


def in_order():
    offsets = list(itertools.product(range(4), range(4), range(2), range(4)))
    rest = offsets[1:]
    def key(o):
        dz, dy, dc, dx = o
        return ((dc - dz & 1) * 4 + (dx - dz - dy & 3)) * 16 + dz * 4 + dy
    rest.sort(key=key)
    return offsets[:1] + rest


ORDER = in_order()
PLACE = np.zeros((8, 128), np.float32)
for at, (oz, oy, oc, ox) in enumerate(ORDER):
    PLACE[:, ((oz * 4 + oy) * 2 + oc) * 4 + ox] = at
PACKED = [
    [sum(ORDER[g * BATCH + i][n] << 2 * g for g in range(BATCHES)) for i in range(BATCH)]
    for n in range(4)
]


def iota(shape, dim):
    return lax.broadcasted_iota(I32, shape, dim)


def kernel(
    owner_hbm,
    face_hbm,
    place_hbm,
    d_hbm,
    m_hbm,
    conduct_hbm,
    casting_hbm,
    mold_hbm,
    volume_hbm,
    cout_v,
    mout_v,
    owner_ref,
    face_ref,
    place_ref,
    d_ref,
    m_ref,
    conduct_ref,
    casting_v,
    mold_v,
    volume_v,
    send_v,
    recv_v,
    ans_v,
    back_v,
    ids_send,
    ids_recv,
    wgap_v,
    mfour_v,
    wcond_v,
    tile_v,
    spread_v,
    row8_v,
    slotrep_v,
    totals_v,
    quarter_v,
    placed_v,
    acc_v,
    load_sem,
    row_sem,
    id_sem,
    ans_sem,
    tot_sem,
    sent_sem,
):
    surf = lax.axis_index("surf")
    x = lax.axis_index("vol")
    z, y, c = surf // 8, lax.rem(surf // 2, 4), lax.rem(surf, 2)

    def peers(g, sign):
        found = []
        for i in range(BATCH):
            if isinstance(g, int):
                dz, dy, dc, dx = ORDER[g * BATCH + i]
            else:
                dz, dy, dc, dx = (packed[i] >> (2 * g) & 3 for packed in PACKED)
            pz, py, pc, px = z + sign * dz & 3, y + sign * dy & 3, c + dc & 1, x + sign * dx & 3
            found.append((((pz * 8 + py * 2 + pc, px)), ((dz * 4 + dy) * 2 + dc) * 4 + dx))
        return found

    def each_peer(g, sign, act, own):
        found = peers(g, sign)
        for i in range(BATCH):
            if i > 0:
                act(g * BATCH + i, *found[i])
            elif isinstance(g, int):
                if g > 0:
                    act(g * BATCH, *found[0])
            else:
                pl.when(g > 0)(functools.partial(act, g * BATCH, *found[0]))
                if own is not None:
                    pl.when(g == 0)(own)

    small = [
        pltpu.make_async_copy(source, place, load_sem.at[4 + n])
        for n, (source, place) in enumerate(
            [
                (owner_hbm, owner_ref),
                (face_hbm, face_ref),
                (place_hbm, place_ref),
                (d_hbm, d_ref),
                (m_hbm, m_ref),
                (conduct_hbm, conduct_ref),
            ]
        )
    ]
    loads = [
        pltpu.make_async_copy(casting_hbm, casting_v, load_sem.at[0]),
        pltpu.make_async_copy(mold_hbm.at[pl.ds(0, 1024)], mold_v.at[:, pl.ds(0, ROW)], load_sem.at[1]),
        pltpu.make_async_copy(mold_hbm.at[pl.ds(1024, 1024)], mold_v.at[:, pl.ds(ROW, ROW)], load_sem.at[2]),
        pltpu.make_async_copy(volume_hbm, volume_v, load_sem.at[3]),
    ]
    for load in small + loads:
        load.start()

    barrier = pltpu.get_barrier_semaphore()

    far_first = sorted(range(1, PEERS), key=lambda j: -hops(ORDER[j]))
    for j in far_first:
        dz, dy, dc, dx = ORDER[j]
        to = ((z + dz & 3) * 8 + (y + dy & 3) * 2 + (c + dc & 1), x + dx & 3)
        pl.semaphore_signal(barrier, inc=1, device_id=to, device_id_type=MESH)

    small[0].wait()
    owner = owner_ref[...]
    dx = (owner & 3) - x & 3
    dc = (owner >> 2 & 1) - c & 1
    dy = (owner >> 3 & 3) - y & 3
    dz = (owner >> 5 & 3) - z & 3
    offset = ((dz * 4 + dy) * 2 + dc) * 4 + dx
    down, lane = iota((ROW, ROW), 0), iota((ROW, ROW), 1)
    before = jnp.concatenate([(down < lane).astype(F32), jnp.ones((ROW, ROW), F32)], axis=1).astype(BF)
    small[2].wait()
    place = place_ref[...].astype(BF)
    hits, sofar = [], jnp.zeros((PEERS, ROW), F32)
    for b in range(8):
        hit = down == offset[b : b + 1, :]
        hits.append(hit.astype(F32).astype(BF))
        count = jnp.dot(hits[b], before, preferred_element_type=F32)
        rank = jnp.sum(jnp.where(hit, count[:, :ROW] + sofar, 0.0), axis=0, keepdims=True)
        sofar = sofar + count[:, ROW:]
        order = jnp.dot(place, hits[b], preferred_element_type=F32)[0:1]
        row8_v[b : b + 1, :] = order * PER + rank
    slot8 = row8_v[...]
    slot_t = slot8.T
    small[1].wait()
    face_t = face_ref[...].astype(F32).T
    table = jnp.zeros((PEERS, ROW), F32)
    for b in range(8):
        slot = jnp.broadcast_to(slot_t[:, b : b + 1], (ROW, ROW)).astype(I32)
        face = jnp.broadcast_to(face_t[:, b : b + 1], (ROW, ROW)).astype(I32)
        slotrep_v[pl.ds(b * ROW, ROW), :] = slot
        part = jnp.where(lane < 32, face & 255, jnp.where(lane < 64, face >> 8 & 3, face >> 10))
        part = jnp.where(((lane & 31) == (slot & 31)) & (lane < 96), part, 0)
        table = table + jnp.dot(hits[b], part.astype(F32).astype(BF), preferred_element_type=F32)
    ids_send[...] = table

    loads[0].wait()

    def pack(g, _):
        want = iota((SLOTS, ROW), 0) + g * SLOTS
        want = want.astype(F32)
        pick = jnp.concatenate(
            [(want == row8_v[b : b + 1, :]).astype(F32).astype(BF) for b in range(8)], axis=1
        )
        rows = jnp.dot(pick, casting_v[...], preferred_element_type=F32).astype(BF)
        send_v[pl.ds(g * BATCH, BATCH)] = rows.reshape(BATCH, PER, ROW)
        return 0

    pack(0, 0)
    pack(1, 0)
    pl.semaphore_wait(barrier, PEERS - 1)

    def send(g, _):
        def one(j, to, k):
            pltpu.make_async_remote_copy(
                src_ref=ids_send.at[pl.ds(k, 1)],
                dst_ref=ids_recv.at[pl.ds(j, 1)],
                send_sem=sent_sem.at[0],
                recv_sem=id_sem.at[g],
                device_id=to,
                device_id_type=MESH,
            ).start()
            pltpu.make_async_remote_copy(
                src_ref=send_v.at[j],
                dst_ref=recv_v.at[j],
                send_sem=sent_sem.at[1],
                recv_sem=row_sem.at[g],
                device_id=to,
                device_id_type=MESH,
            ).start()

        def own():
            pltpu.make_async_copy(ids_send.at[pl.ds(0, 1)], ids_recv.at[pl.ds(0, 1)], id_sem.at[0]).start()
            pltpu.make_async_copy(send_v.at[0], recv_v.at[0], row_sem.at[0]).start()

        each_peer(g, 1, one, own)

        @pl.when(g < BATCHES - 2)
        def _():
            pack(g + 2, 0)

        return 0

    lax.fori_loop(0, BATCHES, send, 0)

    for load in small[3:]:
        load.wait()
    wgap_v[...] = jnp.zeros_like(wgap_v)
    wgap_v[NODES:, 0:NODES] = d_ref[...]
    wgap_v[NODES:, ROW : ROW + NODES] = -m_ref[...]
    mtwo = jnp.concatenate([m_ref[...], m_ref[...]], axis=1)
    mfour_v[...] = jnp.zeros_like(mfour_v)
    mfour_v[NODES:, 0:ROW] = mtwo
    mfour_v[NODES:, ROW:] = mtwo
    for half in range(2):
        pick = jnp.where((down == lane + half * NODES) & (lane < NODES), 0.5, 0.0)
        wcond_v[half, 0:ROW, :] = pick.astype(BF)
        wcond_v[half, ROW:, :] = (conduct_ref[...].astype(F32) * -0.5).astype(BF)
    wide_d, wide_l = iota((ROW, SLOTS), 0), iota((ROW, SLOTS), 1)
    tile = jnp.where(wide_d == (wide_l & 31), 1.0, jnp.where(wide_d == (wide_l & 31) + 64, 256.0, 0.0))
    tile_v[...] = tile.astype(BF)
    down2, lane2 = iota((ROW, 2 * ROW), 0), iota((ROW, 2 * ROW), 1)
    part2 = down2 >> 5
    spread = jnp.where(
        lane2 < ROW,
        jnp.where(part2 == 0, 1.0, jnp.where(part2 == 1, 256.0, 0.0)),
        jnp.where(part2 == 1, 1.0, jnp.where(part2 == 2, 4.0, 0.0)),
    )
    spread_v[...] = spread.astype(BF)
    totals_v[...] = jnp.zeros_like(totals_v)
    acc_v[...] = jnp.zeros_like(acc_v)

    loads[1].wait()
    loads[2].wait()

    def wait_for(ref, sem):
        pltpu.make_async_copy(ref, ref, sem).wait()

    def settle(g, _):
        span = pl.ds(pl.multiple_of(g * BATCH, BATCH), BATCH)
        wait_for(ids_recv.at[span], id_sem.at[g])
        wait_for(recv_v.at[span], row_sem.at[g])
        ids = ids_recv[span, :]
        across = jnp.dot(ids.astype(BF), tile_v[...], preferred_element_type=F32)
        mine = iota((BATCH, SLOTS), 0) == iota((BATCH, SLOTS), 1) >> 5
        across = jnp.sum(jnp.where(mine, across, 0.0), axis=0, keepdims=True)
        keep = iota((PER, ROW), 0) == (iota((PER, ROW), 1) & 31)
        spaced = jnp.where(keep[None], jnp.broadcast_to(ids[:, None, :], (BATCH, PER, ROW)), 0.0)
        spaced = spaced.reshape(SLOTS, ROW).astype(BF)
        both = jnp.dot(spaced, spread_v[...], preferred_element_type=F32)
        low, high = both[:, :ROW], both[:, ROW:]
        lanes = iota((SLOTS, ROW), 1).astype(F32)
        pick = jnp.concatenate([(low - t * ROW == lanes).astype(F32).astype(BF) for t in range(8)], axis=1)
        found = jnp.dot(pick, mold_v[...], preferred_element_type=F32)
        upper = high >= 4.0
        faces = jnp.where(upper, found[:, ROW:], found[:, :ROW]).astype(BF)
        rows = recv_v[span].reshape(SLOTS, ROW)
        pair = jnp.concatenate([rows, faces], axis=1)
        gap = lax.dot_general(pair, wgap_v[...], (((1,), (1,)), ((), ())), preferred_element_type=F32)
        flux = (rows.astype(F32) * faces.astype(F32) * gap).astype(BF)
        back = jnp.dot(flux, wgap_v[:, :ROW], preferred_element_type=F32)
        answer = (back + gap).astype(BF)
        ans_v[span] = answer.reshape(BATCH, PER, ROW)

        def one(j, to, k):
            pltpu.make_async_remote_copy(
                src_ref=ans_v.at[j],
                dst_ref=back_v.at[j],
                send_sem=sent_sem.at[2],
                recv_sem=ans_sem.at[g],
                device_id=to,
                device_id_type=MESH,
            ).start()

        def own():
            pltpu.make_async_copy(ans_v.at[0], back_v.at[0], ans_sem.at[0]).start()

        each_peer(g, -1, one, own)
        gain = jnp.dot(flux, mfour_v[...], preferred_element_type=F32)
        column = jnp.where(upper, high - 4.0, high)
        block = (iota((SLOTS, ROW), 1) >> 6).astype(F32)
        gain = jnp.concatenate(
            [
                jnp.where(column == block, gain[:, :ROW], 0.0).astype(BF),
                jnp.where(column == block + 2.0, gain[:, ROW:], 0.0).astype(BF),
            ],
            axis=1,
        )
        put = (iota((SLOTS, SLOTS), 0).astype(F32) == across).astype(F32).astype(BF)
        totals_v[...] += jnp.dot(put, gain, preferred_element_type=F32)
        return 0

    lax.fori_loop(0, BATCHES, settle, 0)

    for q in range(4):
        rows = slice((q // 2) * 256, (q // 2) * 256 + 256)
        cols = slice((q % 2) * ROW, (q % 2) * ROW + ROW)
        quarter_v[q] = totals_v[rows, cols].astype(BF)
    for d in range(4):
        v = lax.rem(x + d, 4)
        if d == 0:
            pltpu.make_async_copy(quarter_v.at[v], placed_v.at[x], tot_sem.at[0]).start()
        else:
            pltpu.make_async_remote_copy(
                src_ref=quarter_v.at[v],
                dst_ref=placed_v.at[x],
                send_sem=sent_sem.at[3],
                recv_sem=tot_sem.at[0],
                device_id=(surf, v),
                device_id_type=MESH,
            ).start()

    def collect(g, _):
        span = pl.ds(pl.multiple_of(g * BATCH, BATCH), BATCH)
        wait_for(back_v.at[span], ans_sem.at[g])
        lanes = iota((SEGS, ROW), 1) + g * SLOTS
        slots = slotrep_v[...]
        pick = jnp.concatenate(
            [(slots == lanes + t * ROW).astype(F32).astype(BF) for t in range(SLOTS // ROW)], axis=1
        )
        acc_v[...] += jnp.dot(pick, back_v[span].reshape(SLOTS, ROW), preferred_element_type=F32)
        return 0

    lax.fori_loop(0, BATCHES - 2, collect, 0)

    lax.fori_loop(BATCHES - 2, BATCHES, collect, 0)
    cout_v[...] = acc_v[...].astype(BF)
    loads[3].wait()
    wait_for(placed_v, tot_sem.at[0])
    for u in range(4):
        for half in range(2):
            rows = slice(u * QUARTER + half * 256, u * QUARTER + half * 256 + 256)
            volume = volume_v[rows, :]
            both = jnp.concatenate([placed_v[u], volume], axis=1)
            change = jnp.dot(both, wcond_v[half], preferred_element_type=F32)
            mout_v[rows, :] = (volume.astype(F32) + change).astype(BF)

    wait_for(ids_send.at[pl.ds(1, PEERS - 1)], sent_sem.at[0])
    wait_for(send_v.at[pl.ds(1, PEERS - 1)], sent_sem.at[1])
    wait_for(ans_v.at[pl.ds(1, PEERS - 1)], sent_sem.at[2])
    wait_for(quarter_v.at[pl.ds(0, 3)], sent_sem.at[3])


def store(cast_in, mold_in, cast_out, mold_out, sem):
    copies = [
        pltpu.make_async_copy(cast_in, cast_out, sem.at[0]),
        pltpu.make_async_copy(mold_in, mold_out, sem.at[1]),
    ]
    for copy in copies:
        copy.start()
    for copy in copies:
        copy.wait()


def local(casting, owner, face_id, mold_faces, mortar_d, mortar_m, conduct, volume):
    hbm = pl.BlockSpec(memory_space=pltpu.HBM)
    vmem = pl.BlockSpec(memory_space=pltpu.VMEM)
    slots = (PEERS, PER, ROW)
    made = pl.pallas_call(
        kernel,
        out_shape=(
            jax.ShapeDtypeStruct((SEGS, ROW), BF),
            jax.ShapeDtypeStruct((FACES, ROW), BF),
        ),
        in_specs=[hbm] * 9,
        out_specs=(vmem, vmem),
        scratch_shapes=[
            pltpu.VMEM((8, ROW), I32),
            pltpu.VMEM((8, ROW), I32),
            pltpu.VMEM((8, ROW), F32),
            pltpu.VMEM((NODES, NODES), BF),
            pltpu.VMEM((NODES, NODES), BF),
            pltpu.VMEM((ROW, ROW), BF),
            pltpu.VMEM((SEGS, ROW), BF),
            pltpu.VMEM((1024, 2 * ROW), BF),
            pltpu.VMEM((FACES, ROW), BF),
            pltpu.VMEM(slots, BF),
            pltpu.VMEM(slots, BF),
            pltpu.VMEM(slots, BF),
            pltpu.VMEM(slots, BF),
            pltpu.VMEM((PEERS, ROW), F32),
            pltpu.VMEM((PEERS, ROW), F32),
            pltpu.VMEM((ROW, 2 * ROW), BF),
            pltpu.VMEM((ROW, 2 * ROW), BF),
            pltpu.VMEM((2, 2 * ROW, ROW), BF),
            pltpu.VMEM((ROW, SLOTS), BF),
            pltpu.VMEM((ROW, 2 * ROW), BF),
            pltpu.VMEM((8, ROW), F32),
            pltpu.VMEM((SEGS, ROW), I32),
            pltpu.VMEM((SLOTS, 2 * ROW), F32),
            pltpu.VMEM((4, 256, ROW), BF),
            pltpu.VMEM((4, 256, ROW), BF),
            pltpu.VMEM((SEGS, ROW), F32),
            pltpu.SemaphoreType.DMA((10,)),
            pltpu.SemaphoreType.DMA((BATCHES,)),
            pltpu.SemaphoreType.DMA((BATCHES,)),
            pltpu.SemaphoreType.DMA((BATCHES,)),
            pltpu.SemaphoreType.DMA((1,)),
            pltpu.SemaphoreType.DMA((4,)),
        ],
        compiler_params=pltpu.CompilerParams(
            collective_id=0, has_side_effects=True, vmem_limit_bytes=40 * 2**20
        ),
        cost_estimate=pl.CostEstimate(
            flops=2 * 4096 * 1024 * 1024, bytes_accessed=2 * 2**20, transcendentals=0
        ),
    )(
        *(
            pltpu.with_memory_space_constraint(a, pltpu.HBM)
            for a in (
                owner.reshape(8, ROW),
                face_id.reshape(8, ROW),
                jnp.asarray(PLACE),
                mortar_d,
                mortar_m,
                conduct,
                casting,
                mold_faces,
                volume,
            )
        )
    )
    return pl.pallas_call(
        store,
        out_shape=(
            jax.ShapeDtypeStruct((SEGS, ROW), BF),
            jax.ShapeDtypeStruct((FACES, ROW), BF),
        ),
        in_specs=[vmem] * 2,
        out_specs=(hbm, hbm),
        scratch_shapes=[pltpu.SemaphoreType.DMA((2,))],
    )(*(pltpu.with_memory_space_constraint(a, pltpu.VMEM) for a in made))


def solution(mesh):
    rows, flat = P(("surf", "vol"), None), P(("surf", "vol"))
    return jax.shard_map(
        local,
        mesh=mesh,
        in_specs=(rows, rows, flat, rows, P(), P(), P(), rows),
        out_specs=(rows, rows),
        check_vma=False,
    )
```

```python
import functools
import itertools

import jax
import jax.numpy as jnp
import numpy as np
from jax import lax
from jax.experimental import pallas as pl
from jax.experimental.pallas import tpu as pltpu
from jax.sharding import PartitionSpec as P

MESH = pl.DeviceIdType.MESH
BF = jnp.bfloat16
F32 = jnp.float32
I32 = jnp.int32

PEERS = 128
PER = 32
BATCH = 16
BATCHES = PEERS // BATCH
SLOTS = BATCH * PER
NODES = 64
ROW = 128
SEGS = 1024
FACES = 2048
QUARTER = FACES // 4


def hops(offset):
    dz, dy, _, dx = offset
    return sum(min(d, 4 - d) for d in (dz, dy, dx))


def in_order():
    offsets = list(itertools.product(range(4), range(4), range(2), range(4)))
    rest = offsets[1:]
    def key(o):
        dz, dy, dc, dx = o
        return ((dc - dz & 1) * 4 + [0,2,1,3].index(dx - dz - dy & 3)) * 16 + [0,1,2,3].index(dz) * 4 + [0,1,2,3].index(dy)
    rest.sort(key=key)
    return offsets[:1] + rest


ORDER = in_order()
PLACE = np.zeros((8, 128), np.float32)
for at, (oz, oy, oc, ox) in enumerate(ORDER):
    PLACE[:, ((oz * 4 + oy) * 2 + oc) * 4 + ox] = at
PACKED = [
    [sum(ORDER[g * BATCH + i][n] << 2 * g for g in range(BATCHES)) for i in range(BATCH)]
    for n in range(4)
]


def iota(shape, dim):
    return lax.broadcasted_iota(I32, shape, dim)


def kernel(
    owner_hbm,
    face_hbm,
    place_hbm,
    d_hbm,
    m_hbm,
    conduct_hbm,
    casting_hbm,
    mold_hbm,
    volume_hbm,
    cout_v,
    rest_v,
    placed_out,
    owner_ref,
    face_ref,
    place_ref,
    d_ref,
    m_ref,
    conduct_ref,
    casting_v,
    mold_v,
    volume_v,
    send_v,
    recv_v,
    ans_v,
    back_v,
    ids_send,
    ids_recv,
    wgap_v,
    mfour_v,
    cond_v,
    tile_v,
    spread_v,
    row8_v,
    slotrep_v,
    totals_v,
    quarter_v,
    placed_v,
    acc_v,
    load_sem,
    row_sem,
    id_sem,
    ans_sem,
    tot_sem,
    sent_sem,
):
    surf = lax.axis_index("surf")
    x = lax.axis_index("vol")
    z, y, c = surf // 8, lax.rem(surf // 2, 4), lax.rem(surf, 2)

    def peers(g, sign):
        found = []
        for i in range(BATCH):
            if isinstance(g, int):
                dz, dy, dc, dx = ORDER[g * BATCH + i]
            else:
                dz, dy, dc, dx = (packed[i] >> (2 * g) & 3 for packed in PACKED)
            pz, py, pc, px = z + sign * dz & 3, y + sign * dy & 3, c + dc & 1, x + sign * dx & 3
            found.append((((pz * 8 + py * 2 + pc, px)), ((dz * 4 + dy) * 2 + dc) * 4 + dx))
        return found

    def each_peer(g, sign, act, own):
        found = peers(g, sign)
        for i in range(BATCH):
            if i > 0:
                act(g * BATCH + i, *found[i])
            elif isinstance(g, int):
                if g > 0:
                    act(g * BATCH, *found[0])
            else:
                pl.when(g > 0)(functools.partial(act, g * BATCH, *found[0]))
                if own is not None:
                    pl.when(g == 0)(own)

    small = [
        pltpu.make_async_copy(source, place, load_sem.at[4 + n])
        for n, (source, place) in enumerate(
            [
                (owner_hbm, owner_ref),
                (face_hbm, face_ref),
                (place_hbm, place_ref),
                (d_hbm, d_ref),
                (m_hbm, m_ref),
                (conduct_hbm, conduct_ref),
            ]
        )
    ]
    loads = [
        pltpu.make_async_copy(casting_hbm, casting_v, load_sem.at[0]),
        pltpu.make_async_copy(mold_hbm.at[pl.ds(0, 1024)], mold_v.at[:, pl.ds(0, ROW)], load_sem.at[1]),
        pltpu.make_async_copy(mold_hbm.at[pl.ds(1024, 1024)], mold_v.at[:, pl.ds(ROW, ROW)], load_sem.at[2]),
        pltpu.make_async_copy(volume_hbm, volume_v, load_sem.at[3]),
    ]
    for load in small + loads:
        load.start()

    barrier = pltpu.get_barrier_semaphore()

    far_first = sorted(range(1, PEERS), key=lambda j: -hops(ORDER[j]))
    for j in far_first:
        dz, dy, dc, dx = ORDER[j]
        to = ((z + dz & 3) * 8 + (y + dy & 3) * 2 + (c + dc & 1), x + dx & 3)
        pl.semaphore_signal(barrier, inc=1, device_id=to, device_id_type=MESH)

    small[0].wait()
    owner = owner_ref[...]
    dx = (owner & 3) - x & 3
    dc = (owner >> 2 & 1) - c & 1
    dy = (owner >> 3 & 3) - y & 3
    dz = (owner >> 5 & 3) - z & 3
    offset = ((dz * 4 + dy) * 2 + dc) * 4 + dx
    down, lane = iota((ROW, ROW), 0), iota((ROW, ROW), 1)
    before = jnp.concatenate([(down < lane).astype(F32), jnp.ones((ROW, ROW), F32)], axis=1).astype(BF)
    small[2].wait()
    place = place_ref[...].astype(BF)
    hits, sofar = [], jnp.zeros((PEERS, ROW), F32)
    for b in range(8):
        hit = down == offset[b : b + 1, :]
        hits.append(hit.astype(F32).astype(BF))
        count = jnp.dot(hits[b], before, preferred_element_type=F32)
        rank = jnp.sum(jnp.where(hit, count[:, :ROW] + sofar, 0.0), axis=0, keepdims=True)
        sofar = sofar + count[:, ROW:]
        order = jnp.dot(place, hits[b], preferred_element_type=F32)[0:1]
        row8_v[b : b + 1, :] = order * PER + rank
    slot8 = row8_v[...]
    slot_t = slot8.T
    small[1].wait()
    face_t = face_ref[...].astype(F32).T
    table = jnp.zeros((PEERS, ROW), F32)
    for b in range(8):
        slot = jnp.broadcast_to(slot_t[:, b : b + 1], (ROW, ROW)).astype(I32)
        face = jnp.broadcast_to(face_t[:, b : b + 1], (ROW, ROW)).astype(I32)
        slotrep_v[pl.ds(b * ROW, ROW), :] = slot
        part = jnp.where(lane < 32, face & 255, jnp.where(lane < 64, face >> 8 & 3, face >> 10))
        part = jnp.where(((lane & 31) == (slot & 31)) & (lane < 96), part, 0)
        table = table + jnp.dot(hits[b], part.astype(F32).astype(BF), preferred_element_type=F32)
    ids_send[...] = table

    loads[0].wait()

    def pack(g, _):
        want = iota((SLOTS, ROW), 0) + g * SLOTS
        want = want.astype(F32)
        pick = jnp.concatenate(
            [(want == row8_v[b : b + 1, :]).astype(F32).astype(BF) for b in range(8)], axis=1
        )
        rows = jnp.dot(pick, casting_v[...], preferred_element_type=F32).astype(BF)
        send_v[pl.ds(g * BATCH, BATCH)] = rows.reshape(BATCH, PER, ROW)
        return 0

    pack(0, 0)
    pack(1, 0)
    pl.semaphore_wait(barrier, PEERS - 1)

    def send(g, _):
        def one(j, to, k):
            pltpu.make_async_remote_copy(
                src_ref=ids_send.at[pl.ds(k, 1)],
                dst_ref=ids_recv.at[pl.ds(j, 1)],
                send_sem=sent_sem.at[0],
                recv_sem=id_sem.at[g],
                device_id=to,
                device_id_type=MESH,
            ).start()
            pltpu.make_async_remote_copy(
                src_ref=send_v.at[j],
                dst_ref=recv_v.at[j],
                send_sem=sent_sem.at[1],
                recv_sem=row_sem.at[g],
                device_id=to,
                device_id_type=MESH,
            ).start()

        def own():
            pltpu.make_async_copy(ids_send.at[pl.ds(0, 1)], ids_recv.at[pl.ds(0, 1)], id_sem.at[0]).start()
            pltpu.make_async_copy(send_v.at[0], recv_v.at[0], row_sem.at[0]).start()

        each_peer(g, 1, one, own)

        @pl.when(g < BATCHES - 2)
        def _():
            pack(g + 2, 0)

        return 0

    lax.fori_loop(0, BATCHES, send, 0)

    for load in small[3:]:
        load.wait()
    wgap_v[...] = jnp.zeros_like(wgap_v)
    wgap_v[NODES:, 0:NODES] = d_ref[...]
    wgap_v[NODES:, ROW : ROW + NODES] = -m_ref[...]
    mtwo = jnp.concatenate([m_ref[...], m_ref[...]], axis=1)
    mfour_v[...] = jnp.zeros_like(mfour_v)
    mfour_v[NODES:, 0:ROW] = mtwo
    mfour_v[NODES:, ROW:] = mtwo
    cond_v[...] = (conduct_ref[...].astype(F32) * -0.5).astype(BF)
    wide_d, wide_l = iota((ROW, SLOTS), 0), iota((ROW, SLOTS), 1)
    tile = jnp.where(wide_d == (wide_l & 31), 1.0, jnp.where(wide_d == (wide_l & 31) + 64, 256.0, 0.0))
    tile_v[...] = tile.astype(BF)
    down2, lane2 = iota((ROW, 2 * ROW), 0), iota((ROW, 2 * ROW), 1)
    part2 = down2 >> 5
    spread = jnp.where(
        lane2 < ROW,
        jnp.where(part2 == 0, 1.0, jnp.where(part2 == 1, 256.0, 0.0)),
        jnp.where(part2 == 1, 1.0, jnp.where(part2 == 2, 4.0, 0.0)),
    )
    spread_v[...] = spread.astype(BF)
    totals_v[...] = jnp.zeros_like(totals_v)
    acc_v[...] = jnp.zeros_like(acc_v)

    loads[1].wait()
    loads[2].wait()

    def wait_for(ref, sem):
        pltpu.make_async_copy(ref, ref, sem).wait()

    def settle(g, _):
        span = pl.ds(pl.multiple_of(g * BATCH, BATCH), BATCH)
        wait_for(ids_recv.at[span], id_sem.at[g])
        wait_for(recv_v.at[span], row_sem.at[g])
        ids = ids_recv[span, :]
        across = jnp.dot(ids.astype(BF), tile_v[...], preferred_element_type=F32)
        mine = iota((BATCH, SLOTS), 0) == iota((BATCH, SLOTS), 1) >> 5
        across = jnp.sum(jnp.where(mine, across, 0.0), axis=0, keepdims=True)
        keep = iota((PER, ROW), 0) == (iota((PER, ROW), 1) & 31)
        spaced = jnp.where(keep[None], jnp.broadcast_to(ids[:, None, :], (BATCH, PER, ROW)), 0.0)
        spaced = spaced.reshape(SLOTS, ROW).astype(BF)
        both = jnp.dot(spaced, spread_v[...], preferred_element_type=F32)
        low, high = both[:, :ROW], both[:, ROW:]
        lanes = iota((SLOTS, ROW), 1).astype(F32)
        pick = jnp.concatenate([(low - t * ROW == lanes).astype(F32).astype(BF) for t in range(8)], axis=1)
        found = jnp.dot(pick, mold_v[...], preferred_element_type=F32)
        upper = high >= 4.0
        faces = jnp.where(upper, found[:, ROW:], found[:, :ROW]).astype(BF)
        rows = recv_v[span].reshape(SLOTS, ROW)
        pair = jnp.concatenate([rows, faces], axis=1)
        gap = lax.dot_general(pair, wgap_v[...], (((1,), (1,)), ((), ())), preferred_element_type=F32)
        flux = (rows.astype(F32) * faces.astype(F32) * gap).astype(BF)
        back = jnp.dot(flux, wgap_v[:, :ROW], preferred_element_type=F32)
        answer = (back + gap).astype(BF)
        ans_v[span] = answer.reshape(BATCH, PER, ROW)

        def one(j, to, k):
            pltpu.make_async_remote_copy(
                src_ref=ans_v.at[j],
                dst_ref=back_v.at[j],
                send_sem=sent_sem.at[2],
                recv_sem=ans_sem.at[g],
                device_id=to,
                device_id_type=MESH,
            ).start()

        def own():
            pltpu.make_async_copy(ans_v.at[0], back_v.at[0], ans_sem.at[0]).start()

        each_peer(g, -1, one, own)
        gain = jnp.dot(flux, mfour_v[...], preferred_element_type=F32)
        column = jnp.where(upper, high - 4.0, high)
        block = (iota((SLOTS, ROW), 1) >> 6).astype(F32)
        gain = jnp.concatenate(
            [
                jnp.where(column == block, gain[:, :ROW], 0.0).astype(BF),
                jnp.where(column == block + 2.0, gain[:, ROW:], 0.0).astype(BF),
            ],
            axis=1,
        )
        put = (iota((SLOTS, SLOTS), 0).astype(F32) == across).astype(F32).astype(BF)
        totals_v[...] += jnp.dot(put, gain, preferred_element_type=F32)
        return 0

    lax.fori_loop(0, BATCHES, settle, 0)

    for q in range(4):
        rows = slice((q // 2) * 256, (q // 2) * 256 + 256)
        cols = slice((q % 2) * ROW, (q % 2) * ROW + ROW)
        quarter_v[q] = totals_v[rows, cols].astype(BF)
    for d in range(4):
        v = lax.rem(x + d, 4)
        if d == 0:
            pltpu.make_async_copy(quarter_v.at[v], placed_v.at[x], tot_sem.at[0]).start()
        else:
            pltpu.make_async_remote_copy(
                src_ref=quarter_v.at[v],
                dst_ref=placed_v.at[x],
                send_sem=sent_sem.at[3],
                recv_sem=tot_sem.at[0],
                device_id=(surf, v),
                device_id_type=MESH,
            ).start()

    def collect(g, _):
        span = pl.ds(pl.multiple_of(g * BATCH, BATCH), BATCH)
        wait_for(back_v.at[span], ans_sem.at[g])
        lanes = iota((SEGS, ROW), 1) + g * SLOTS
        slots = slotrep_v[...]
        pick = jnp.concatenate(
            [(slots == lanes + t * ROW).astype(F32).astype(BF) for t in range(SLOTS // ROW)], axis=1
        )
        acc_v[...] += jnp.dot(pick, back_v[span].reshape(SLOTS, ROW), preferred_element_type=F32)
        return 0

    loads[3].wait()

    def cool(n, _):
        rows = pl.ds(pl.multiple_of(n * 256, 256), 256)
        volume = volume_v[rows, :]
        rest_v[rows, :] = volume.astype(F32) + jnp.dot(volume, cond_v[...], preferred_element_type=F32)
        return 0

    lax.fori_loop(0, FACES // 256, cool, 0)
    lax.fori_loop(0, BATCHES, collect, 0)
    cout_v[...] = acc_v[...].astype(BF)
    wait_for(placed_v, tot_sem.at[0])
    placed_out[...] = placed_v[...]
    wait_for(ids_send.at[pl.ds(1, PEERS - 1)], sent_sem.at[0])
    wait_for(send_v.at[pl.ds(1, PEERS - 1)], sent_sem.at[1])
    wait_for(ans_v.at[pl.ds(1, PEERS - 1)], sent_sem.at[2])
    wait_for(quarter_v.at[pl.ds(0, 3)], sent_sem.at[3])


def finish(cast_in, rest_in, placed_in, cast_out, mold_out, mold_v, sem):
    stores = [pltpu.make_async_copy(cast_in, cast_out, sem.at[0])]
    stores[0].start()
    down, lane = iota((ROW, ROW), 0), iota((ROW, ROW), 1)
    pick = [
        jnp.where((down == lane + half * NODES) & (lane < NODES), 0.5, 0.0).astype(BF) for half in range(2)
    ]
    for n in range(FACES // 256):
        rows = pl.ds(n * 256, 256)
        heat = jnp.dot(placed_in[n // 2], pick[n % 2], preferred_element_type=F32)
        mold_v[rows, :] = (rest_in[rows, :] + heat).astype(BF)
        if n % 2:
            rows = pl.ds((n - 1) * 256, 512)
            stores.append(pltpu.make_async_copy(mold_v.at[rows], mold_out.at[rows], sem.at[len(stores)]))
            stores[-1].start()
    for copy in stores:
        copy.wait()


def local(casting, owner, face_id, mold_faces, mortar_d, mortar_m, conduct, volume):
    hbm = pl.BlockSpec(memory_space=pltpu.HBM)
    vmem = pl.BlockSpec(memory_space=pltpu.VMEM)
    slots = (PEERS, PER, ROW)
    made = pl.pallas_call(
        kernel,
        out_shape=(
            jax.ShapeDtypeStruct((SEGS, ROW), BF),
            jax.ShapeDtypeStruct((FACES, ROW), F32),
            jax.ShapeDtypeStruct((4, 256, ROW), BF),
        ),
        in_specs=[hbm] * 9,
        out_specs=(vmem, vmem, vmem),
        scratch_shapes=[
            pltpu.VMEM((8, ROW), I32),
            pltpu.VMEM((8, ROW), I32),
            pltpu.VMEM((8, ROW), F32),
            pltpu.VMEM((NODES, NODES), BF),
            pltpu.VMEM((NODES, NODES), BF),
            pltpu.VMEM((ROW, ROW), BF),
            pltpu.VMEM((SEGS, ROW), BF),
            pltpu.VMEM((1024, 2 * ROW), BF),
            pltpu.VMEM((FACES, ROW), BF),
            pltpu.VMEM(slots, BF),
            pltpu.VMEM(slots, BF),
            pltpu.VMEM(slots, BF),
            pltpu.VMEM(slots, BF),
            pltpu.VMEM((PEERS, ROW), F32),
            pltpu.VMEM((PEERS, ROW), F32),
            pltpu.VMEM((ROW, 2 * ROW), BF),
            pltpu.VMEM((ROW, 2 * ROW), BF),
            pltpu.VMEM((ROW, ROW), BF),
            pltpu.VMEM((ROW, SLOTS), BF),
            pltpu.VMEM((ROW, 2 * ROW), BF),
            pltpu.VMEM((8, ROW), F32),
            pltpu.VMEM((SEGS, ROW), I32),
            pltpu.VMEM((SLOTS, 2 * ROW), F32),
            pltpu.VMEM((4, 256, ROW), BF),
            pltpu.VMEM((4, 256, ROW), BF),
            pltpu.VMEM((SEGS, ROW), F32),
            pltpu.SemaphoreType.DMA((10,)),
            pltpu.SemaphoreType.DMA((BATCHES,)),
            pltpu.SemaphoreType.DMA((BATCHES,)),
            pltpu.SemaphoreType.DMA((BATCHES,)),
            pltpu.SemaphoreType.DMA((1,)),
            pltpu.SemaphoreType.DMA((4,)),
        ],
        compiler_params=pltpu.CompilerParams(
            collective_id=0, has_side_effects=True, vmem_limit_bytes=40 * 2**20
        ),
        cost_estimate=pl.CostEstimate(
            flops=2 * 4096 * 1024 * 1024, bytes_accessed=2 * 2**20, transcendentals=0
        ),
    )(
        *(
            pltpu.with_memory_space_constraint(a, pltpu.HBM)
            for a in (
                owner.reshape(8, ROW),
                face_id.reshape(8, ROW),
                jnp.asarray(PLACE),
                mortar_d,
                mortar_m,
                conduct,
                casting,
                mold_faces,
                volume,
            )
        )
    )
    return pl.pallas_call(
        finish,
        out_shape=(
            jax.ShapeDtypeStruct((SEGS, ROW), BF),
            jax.ShapeDtypeStruct((FACES, ROW), BF),
        ),
        in_specs=[vmem] * 3,
        out_specs=(hbm, hbm),
        scratch_shapes=[pltpu.VMEM((FACES, ROW), BF), pltpu.SemaphoreType.DMA((5,))],
    )(*(pltpu.with_memory_space_constraint(a, pltpu.VMEM) for a in made))


def solution(mesh):
    rows, flat = P(("surf", "vol"), None), P(("surf", "vol"))
    return jax.shard_map(
        local,
        mesh=mesh,
        in_specs=(rows, rows, flat, rows, P(), P(), P(), rows),
        out_specs=(rows, rows),
        check_vma=False,
    )
```
